256 devices in a mesh: ctx: 128 (over x, z, y_lo, core), head: 2 (over y_hi).
Axes of the slice: x: 4, y: 4 (y_hi: 2, y_lo: 2; y = y_hi * 2 + y_lo), z: 8, core: 2. Of those that a mesh axis runs over, the one named last changes fastest.
Arguments:
- queries: bfloat16 [32768, 4096], P('ctx', 'head')
- keys: bfloat16 [32768, 256], P('ctx', 'head')
- values: bfloat16 [32768, 256], P('ctx', 'head'), may hold values from -6 to 6
- comp_keys: bfloat16 [512, 256], P('ctx', 'head')
- comp_values: bfloat16 [512, 256], P('ctx', 'head'), may hold values from -6 to 6
- selected: int32 [512, 15], replicated, may hold values from -1 to 507, as said below
- inputs: bfloat16 [32768, 2560], P('ctx'), may hold values from -6 to 6
- w_gate: bfloat16 [2560, 64], P(None, 'head'), may hold values from -0.125 to 0.125
- d_out: bfloat16 [32768, 4096], P('ctx', 'head'), may hold values from -6 to 6
Outputs:
- d_queries: bfloat16 [32768, 4096], P('ctx', 'head')
- d_keys: bfloat16 [32768, 256], P('ctx', 'head')
- d_values: bfloat16 [32768, 256], P('ctx', 'head')
- d_comp_keys: bfloat16 [512, 256], P('ctx', 'head')
- d_comp_values: bfloat16 [512, 256], P('ctx', 'head')
- d_inputs: bfloat16 [32768, 2560], P('ctx', 'head')
The draws below stay inside these ranges and needn't reach their ends.
Inputs may be any that keep to these rules, and one draw needn't show every extreme that they name: `selected`: block c lies on index c // 4 of ctx. Let H = 128 // 2. Entry j of row b names a block on the index that lies r places before the index holding block b, where r = 1 + j * max(H - 1, 0) // 14 for even b and r = H + 1 + j * max(H - 2, 0) // 14 for odd b; the entry is -1 where that index would be below 0 or where r equals that of entry j - 1 of the same row. Over the 4 rows of one index of ctx, each index that is named is named exactly 2 times.
All inputs are finite; a program needn't handle non-finite values.
Results may differ from the reference program's by a relative error of at most 0.019.
Values may be sent and summed in bfloat16 or wider, within the bound.
A program may use at most 128 MiB of HBM per device.

```python
import jax
import jax.numpy as jnp
from jax import lax

D = 2560
HD = 128
HEADS = 16
BLK = 64
PICKS = 15
GROUPS = 2
QB = 4
TOKENS = 32768
NBLK = 512


def draw_queries(key, part):
    own_key = jax.random.fold_in(key, 1)
    shape = (TOKENS, GROUPS * HEADS * HD)
    result = jnp.clip(jax.random.normal(own_key, shape, jnp.float32), -6.0, 6.0)
    return result.astype(jnp.bfloat16)


def draw_keys(key, part):
    own_key = jax.random.fold_in(key, 2)
    shape = (TOKENS, GROUPS * HD)
    result = jnp.clip(jax.random.normal(own_key, shape, jnp.float32), -6.0, 6.0)
    return result.astype(jnp.bfloat16)


def draw_comp_keys(key, part):
    own_key = jax.random.fold_in(key, 3)
    shape = (NBLK, GROUPS * HD)
    result = jnp.clip(jax.random.normal(own_key, shape, jnp.float32), -6.0, 6.0)
    return result.astype(jnp.bfloat16)


def reach_table(ranks, parity, column):
    half = ranks // 2
    near = 1 + column * max(half - 1, 0) // (PICKS - 1)
    far = half + 1 + column * max(half - 2, 0) // (PICKS - 1)
    return jnp.where(parity == 1, far, near)


def draw_selected(key, part):
    ranks = NBLK // QB
    device = jnp.arange(ranks, dtype=jnp.int32)[:, None, None]
    rowpos = jnp.arange(QB, dtype=jnp.int32)[None, :, None]
    parity = rowpos % 2
    column = jnp.arange(PICKS, dtype=jnp.int32)[None, None, :]
    reach = reach_table(ranks, parity, column)
    before = reach_table(ranks, parity, jnp.maximum(column - 1, 0))
    repeated = (column > 0) & (reach == before)
    owner = device - reach
    local = jax.random.randint(jax.random.fold_in(key, 12), (ranks, QB, PICKS), 0, QB)
    top_entry = (device == ranks - 1) & (rowpos == 0) & (column == 0)
    local = jnp.where(top_entry, QB - 1, local)
    picks = jnp.where((owner >= 0) & jnp.logical_not(repeated), owner * QB + local, -1)
    return picks.reshape(NBLK, PICKS).astype(jnp.int32)


def level_of(key, dims, shards, smallest, top_value):
    def one(position, parts):
        steps = jax.random.uniform(jax.random.fold_in(jax.random.fold_in(key, 6), position), (parts,), jnp.float32, smallest / len(shards), top_value / len(shards))
        return jnp.repeat(jnp.exp(steps), dims[position] // parts).reshape((-1,) + (1,) * (len(dims) - position - 1))

    gain = one(*shards[0])
    for cut in shards[1:]:
        gain = gain * one(*cut)
    return gain


def centred(key, shape, width, limit, cuts=(), held_as=jnp.bfloat16):
    factor_of = level_of(key, shape, cuts, -0.22, 0.18) if cuts else 1.0
    values = jax.random.normal(key, shape, jnp.float32) * width * factor_of
    return jnp.minimum(jnp.maximum(values, -limit), limit).astype(held_as)


def setup_inputs(seed: int = 0) -> dict:
    arg_keys = jax.random.split(jax.random.key(seed), 10)
    return {
        "queries": draw_queries(jax.random.fold_in(arg_keys[9], 71), 0),
        "keys": draw_keys(jax.random.fold_in(arg_keys[9], 71), 0),
        "values": centred(arg_keys[2], (TOKENS, GROUPS * HD), 1.0, 6.0, ((0, 128), (1, 2))),
        "comp_keys": draw_comp_keys(jax.random.fold_in(arg_keys[9], 71), 0),
        "comp_values": centred(arg_keys[4], (NBLK, GROUPS * HD), 1.0, 6.0, ((0, 128), (1, 2))),
        "selected": draw_selected(jax.random.fold_in(arg_keys[9], 71), 0),
        "inputs": centred(arg_keys[6], (TOKENS, D), 1.0, 6.0, ((0, 128),)),
        "w_gate": centred(arg_keys[7], (D, GROUPS * 2 * HEADS), D ** -0.5, 0.125, ((1, 2),)),
        "d_out": centred(arg_keys[8], (TOKENS, GROUPS * HEADS * HD), 1.0, 6.0, ((0, 128), (1, 2))),
    }


def attend(query_blk, key_set, value_set, visible, dout_blk, gate_blk):
    scale = HD ** -0.5
    scores = jnp.einsum('thd,kd->thk', query_blk.astype(jnp.float32), key_set.astype(jnp.float32)) * scale
    scores = jnp.where(visible[:, None, :], scores, -jnp.inf)
    top = jnp.max(scores, axis=-1, keepdims=True)
    expo = jnp.exp(scores - top)
    probs = (expo / jnp.sum(expo, axis=-1, keepdims=True)).astype(jnp.bfloat16)
    out = jnp.einsum('thk,kd->thd', probs.astype(jnp.float32), value_set.astype(jnp.float32))
    d_gate = jnp.sum(dout_blk.astype(jnp.float32) * out, axis=-1)
    d_branch = (gate_blk[:, :, None] * dout_blk.astype(jnp.float32)).astype(jnp.bfloat16)
    d_prob = jnp.einsum('thd,kd->thk', d_branch.astype(jnp.float32), value_set.astype(jnp.float32))
    delta = jnp.sum(probs.astype(jnp.float32) * d_prob, axis=-1, keepdims=True)
    d_score = (probs.astype(jnp.float32) * (d_prob - delta) * scale).astype(jnp.bfloat16)
    d_query = jnp.einsum('thk,kd->thd', d_score.astype(jnp.float32), key_set.astype(jnp.float32))
    d_key = jnp.einsum('thk,thd->kd', d_score.astype(jnp.float32), query_blk.astype(jnp.float32))
    d_value = jnp.einsum('thk,thd->kd', probs.astype(jnp.float32), d_branch.astype(jnp.float32))
    return d_query, d_key, d_value, d_gate


def reference(queries, keys, values, comp_keys, comp_values, selected, inputs, w_gate, d_out):
    gate = jax.nn.sigmoid(jnp.dot(inputs, w_gate, preferred_element_type=jnp.float32))
    lower = jnp.arange(BLK)[:, None] >= jnp.arange(BLK)[None, :]
    dq_parts, dk_parts, dv_parts, dck_parts, dcv_parts, dgate_parts = [], [], [], [], [], []
    for group in range(GROUPS):
        qsel = queries[:, group * HEADS * HD:(group + 1) * HEADS * HD].reshape(NBLK, BLK, HEADS, HD)
        dsel = d_out[:, group * HEADS * HD:(group + 1) * HEADS * HD].reshape(NBLK, BLK, HEADS, HD)
        kblocks = keys[:, group * HD:(group + 1) * HD].reshape(NBLK, BLK, HD)
        vblocks = values[:, group * HD:(group + 1) * HD].reshape(NBLK, BLK, HD)
        ckeys = comp_keys[:, group * HD:(group + 1) * HD]
        cvals = comp_values[:, group * HD:(group + 1) * HD]
        gates = gate[:, group * 2 * HEADS:(group + 1) * 2 * HEADS].reshape(NBLK, BLK, 2 * HEADS)

        def step(carry, block):
            dk_acc, dv_acc, dck_acc, dcv_acc = carry
            query_blk = qsel[block]
            dout_blk = dsel[block]
            gate_blk = gates[block]
            pos = block * BLK + jnp.arange(BLK, dtype=jnp.int32)
            vis_c = (jnp.arange(NBLK, dtype=jnp.int32)[None, :] * BLK) <= pos[:, None]
            dqc, dckb, dcvb, dgc = attend(query_blk, ckeys, cvals, vis_c, dout_blk, gate_blk[:, :HEADS])
            row = selected[block]
            valid = row >= 0
            index = jnp.where(valid, row, 0).astype(jnp.int32)
            key_set = jnp.concatenate([kblocks[block][None], kblocks[index]], axis=0).reshape((PICKS + 1) * BLK, HD)
            value_set = jnp.concatenate([vblocks[block][None], vblocks[index]], axis=0).reshape((PICKS + 1) * BLK, HD)
            vis_p = jnp.broadcast_to(jnp.repeat(valid, BLK)[None, :], (BLK, PICKS * BLK))
            vis_s = jnp.concatenate([lower, vis_p], axis=1)
            dqs, dks, dvs, dgs = attend(query_blk, key_set, value_set, vis_s, dout_blk, gate_blk[:, HEADS:])
            dks = dks.reshape(PICKS + 1, BLK, HD)
            dvs = dvs.reshape(PICKS + 1, BLK, HD)
            weight = valid.astype(jnp.float32)[:, None, None]
            dk_acc = dk_acc.at[block].add(dks[0]).at[index].add(dks[1:] * weight)
            dv_acc = dv_acc.at[block].add(dvs[0]).at[index].add(dvs[1:] * weight)
            d_query = (dqc + dqs).reshape(BLK, HEADS * HD).astype(jnp.bfloat16)
            d_gate = jnp.concatenate([dgc, dgs], axis=-1)
            return (dk_acc, dv_acc, dck_acc + dckb, dcv_acc + dcvb), (d_query, d_gate)

        start = (jnp.zeros((NBLK, BLK, HD), jnp.float32), jnp.zeros((NBLK, BLK, HD), jnp.float32),
                 jnp.zeros((NBLK, HD), jnp.float32), jnp.zeros((NBLK, HD), jnp.float32))
        carry, outs = lax.scan(step, start, jnp.arange(NBLK, dtype=jnp.int32))
        dq_parts.append(outs[0].reshape(TOKENS, HEADS * HD))
        dgate_parts.append(outs[1].reshape(TOKENS, 2 * HEADS))
        dk_parts.append(carry[0].reshape(TOKENS, HD))
        dv_parts.append(carry[1].reshape(TOKENS, HD))
        dck_parts.append(carry[2])
        dcv_parts.append(carry[3])
    d_gate = jnp.concatenate(dgate_parts, axis=1)
    d_z = (d_gate * gate * (1.0 - gate)).astype(jnp.bfloat16)
    d_inputs = lax.dot_general(d_z, w_gate, (((1,), (1,)), ((), ())), preferred_element_type=jnp.float32)
    return (jnp.concatenate(dq_parts, axis=1),
            jnp.concatenate(dk_parts, axis=1).astype(jnp.bfloat16),
            jnp.concatenate(dv_parts, axis=1).astype(jnp.bfloat16),
            jnp.concatenate(dck_parts, axis=1).astype(jnp.bfloat16),
            jnp.concatenate(dcv_parts, axis=1).astype(jnp.bfloat16),
            d_inputs.astype(jnp.bfloat16))
```

```python
import functools

import jax
import jax.numpy as jnp
from jax import lax
from jax.experimental import pallas as pl
from jax.experimental.pallas import tpu as pltpu
from jax.sharding import PartitionSpec as P

BLK = 64
PICKS = 15
HD = 128
QB = 4
RANKS = 128
HEADS = 16
LOW = 16
OUTER = RANKS // LOW
HALF = RANKS // 2
SCALE = HD ** -0.5
LOG2E = 1.4426950408889634
BF = jnp.bfloat16
F32 = jnp.float32
MIB = 1 << 20


def reach(parity, j):
    if parity == 0:
        return 1 + (j * (HALF - 1)) // (PICKS - 1)
    return HALF + 1 + (j * (HALF - 2)) // (PICKS - 1)


REACH = [(p, j, reach(p, j)) for p in range(2) for j in range(PICKS)]


def count(conditions):
    return sum(c.astype(jnp.int32) for c in conditions)


def at_ctx(index):
    return {"ctx": index}


def signal(sem, device):
    pl.semaphore_signal(sem, inc=1, device_id=device, device_id_type=pl.DeviceIdType.MESH)


def remote(src, dst, send_sem, recv_sem, device):
    return pltpu.make_async_remote_copy(
        src_ref=src,
        dst_ref=dst,
        send_sem=send_sem,
        recv_sem=recv_sem,
        device_id=device,
        device_id_type=pl.DeviceIdType.MESH,
    )


def fetch_kernel(
    sel_ref, k_ref, v_ref, ck_ref, cv_ref, w_ref,
    kv_ref, comp_ref, wother_ref,
    out_buf, kv_send, kv_recv, a_send, a_recv, b_send, b_recv, w_sems,
):
    me = lax.axis_index("ctx")
    hd = lax.axis_index("head")
    group = me // LOW
    low = me % LOW
    partner = {"head": 1 - hd}

    barrier = pltpu.get_barrier_semaphore()
    for a in range(LOW):
        @pl.when(a != low)
        def _():
            signal(barrier, at_ctx(group * LOW + a))
    for p, j, r in REACH:
        @pl.when(me >= r)
        def _():
            signal(barrier, at_ctx(me - r))
    for g in range(OUTER):
        @pl.when(g < group)
        def _():
            signal(barrier, at_ctx(g * LOW + low))
    signal(barrier, partner)

    comp_ref[pl.ds(me, 1), 0:4, :] = ck_ref[...].astype(F32)[None]
    comp_ref[pl.ds(me, 1), 4:8, :] = cv_ref[...].astype(F32)[None]
    for g in range(OUTER):
        @pl.when(g > group)
        def _():
            comp_ref[g * LOW:(g + 1) * LOW] = jnp.zeros((LOW, 8, HD), F32)
    for p, j, r in REACH:
        slot = p * PICKS + j
        asker = jnp.minimum(me + r, RANKS - 1)
        for i in range(2):
            local = sel_ref[(asker * QB + p + 2 * i) * PICKS + j] & (QB - 1)
            out_buf[slot, i, :, 0:HD] = k_ref[local]
            out_buf[slot, i, :, HD:] = v_ref[local]
        @pl.when(me < r)
        def _():
            kv_ref[:, p, j] = jnp.zeros((2, BLK, 2 * HD), BF)
    for b in range(QB):
        kv_ref[b // 2, b % 2, PICKS, :, 0:HD] = k_ref[b]
        kv_ref[b // 2, b % 2, PICKS, :, HD:] = v_ref[b]

    askers = count([me + r < RANKS for _, _, r in REACH])
    pl.semaphore_wait(barrier, askers + (LOW - 1) + (OUTER - 1 - group) + 1)

    def a_copy(a, slot):
        return remote(
            comp_ref.at[slot], comp_ref.at[slot], a_send.at[a], a_recv.at[slot % LOW],
            at_ctx(group * LOW + a),
        )

    def kv_copy(p, j, r, target):
        slot = p * PICKS + j
        return remote(
            out_buf.at[slot], kv_ref.at[:, p, j], kv_send.at[slot], kv_recv.at[slot],
            at_ctx(target),
        )

    def b_copy(g, source):
        rows = pl.ds(source * LOW, LOW)
        return remote(
            comp_ref.at[rows], comp_ref.at[rows], b_send.at[g], b_recv.at[source],
            at_ctx(g * LOW + low),
        )

    w_copy = remote(w_ref.at[1 - hd], wother_ref, w_sems.at[0], w_sems.at[1], partner)

    for a in range(LOW):
        @pl.when(a != low)
        def _():
            a_copy(a, me).start()
    for p, j, r in REACH:
        @pl.when(me + r < RANKS)
        def _():
            kv_copy(p, j, r, me + r).start()
    w_copy.start()
    for a in range(LOW):
        @pl.when(a != low)
        def _():
            a_copy(a, group * LOW + a).wait_recv()
    for g in range(OUTER):
        @pl.when(g > group)
        def _():
            b_copy(g, group).start()
    for g in range(OUTER):
        @pl.when(g < group)
        def _():
            b_copy(g, g).wait_recv()
    for p, j, r in REACH:
        @pl.when(me >= r)
        def _():
            kv_copy(p, j, r, me - r).wait_recv()
    w_copy.wait_recv()
    for a in range(LOW):
        @pl.when(a != low)
        def _():
            a_copy(a, me).wait_send()
    for p, j, r in REACH:
        @pl.when(me + r < RANKS)
        def _():
            kv_copy(p, j, r, me + r).wait_send()
    for g in range(OUTER):
        @pl.when(g > group)
        def _():
            b_copy(g, group).wait_send()
    w_copy.wait_send()


def nt(a, b):
    return lax.dot_general(a, b, (((1,), (1,)), ((), ())), preferred_element_type=F32)


def nn(a, b):
    return lax.dot_general(a, b, (((1,), (0,)), ((), ())), preferred_element_type=F32)


def scores_backward(k, v, kt, bias, q, do):
    s = nt(k, q) * (SCALE * LOG2E) + bias
    top = jnp.max(s, axis=0, keepdims=True)
    e = jnp.exp2(s - top)
    prob = e * (1.0 / jnp.sum(e, axis=0, keepdims=True))
    dp = nt(v, do)
    delta = jnp.sum(prob * dp, axis=0, keepdims=True)
    ds = (prob * (dp - delta)).astype(BF)
    dv = nn(prob.astype(BF), do)
    dk = nn(ds, q)
    dqt = nn(kt, ds)
    return dqt, dk, dv, delta


def local_kernel(
    q_ref, do_ref, x_ref, w_ref, kv_ref, comp_ref,
    dq_ref, dkv_ref, down_ref, dcomp_ref, dz_ref,
    doc, dos, dq_acc, bias_c, bias_s, ck, cv, ckt, kt, dc_acc, dkv_acc, delta_c, delta_s,
):
    me = lax.axis_index("ctx")
    tokens = q_ref.shape[0]
    half = w_ref.shape[2]

    x0, x1 = x_ref[:, 0:half], x_ref[:, half:]
    gate = jax.nn.sigmoid(nt(x0, w_ref[0]) + nt(x1, w_ref[1]))
    for h in range(HEADS):
        slab = do_ref[:, h * HD:(h + 1) * HD].astype(F32)
        doc[:, h * HD:(h + 1) * HD] = (gate[:, h:h + 1] * slab).astype(BF)
        dos[:, h * HD:(h + 1) * HD] = (gate[:, HEADS + h:HEADS + h + 1] * slab).astype(BF)

    pairs = comp_ref[...].reshape(RANKS // 2, 2, 8, HD)
    even, odd = pairs[:, 0], pairs[:, 1]
    top_rows = lax.broadcasted_iota(jnp.int32, (RANKS // 2, 8, HD), 1) < 4
    swap = lambda z: pltpu.roll(z, 4, 1)
    keys_c = jnp.where(top_rows, even, swap(odd)).reshape(RANKS * 4, HD)
    vals_c = jnp.where(top_rows, swap(even), odd).reshape(RANKS * 4, HD)
    ck[...] = keys_c.astype(BF)
    cv[...] = vals_c.astype(BF)
    ckt[...] = keys_c.T.astype(BF)

    row = lax.broadcasted_iota(jnp.int32, (RANKS * QB, tokens), 0)
    col = lax.broadcasted_iota(jnp.int32, (RANKS * QB, tokens), 1)
    bias_c[...] = jnp.where(row <= me * QB + col // BLK, 0.0, -jnp.inf)
    srow = lax.broadcasted_iota(jnp.int32, (BLK, 4 * BLK), 0)
    scol = lax.broadcasted_iota(jnp.int32, (BLK, 4 * BLK), 1) % BLK
    own_bias = jnp.where(srow <= scol, 0.0, -jnp.inf)
    for p, j, r in REACH:
        bias_s[p, j * BLK:(j + 1) * BLK, :] = jnp.full(
            (BLK, 4 * BLK), jnp.where(me >= r, 0.0, -jnp.inf), F32
        )
    for p in range(2):
        bias_s[p, PICKS * BLK:, :] = own_bias

    dc_acc[...] = jnp.zeros_like(dc_acc)

    def comp_head(h, carry):
        lanes = pl.ds(pl.multiple_of(h * HD, HD), HD)
        dqt, dk, dv, delta = scores_backward(
            ck[...], cv[...], ckt[...], bias_c[...], q_ref[:, lanes], doc[:, lanes]
        )
        dq_acc[:, lanes] = dqt.T
        dc_acc[0] += dk
        dc_acc[1] += dv
        delta_c[pl.ds(h, 1), :] = delta
        return carry

    lax.fori_loop(0, HEADS, comp_head, 0)

    def sel_block(b, carry):
        rows = pl.ds(pl.multiple_of(b * BLK, BLK), BLK)
        kt[...] = kv_ref[b, :, 0:HD].astype(F32).T.astype(BF)
        dkv_acc[...] = jnp.zeros_like(dkv_acc)
        bias = bias_s.at[lax.rem(b, 2)]

        def heads4(g, inner):
            lanes = [pl.ds(pl.multiple_of((g + 4 * i) * HD, HD), HD) for i in range(4)]
            q = jnp.concatenate([q_ref[rows, l] for l in lanes], axis=0)
            do = jnp.concatenate([dos[rows, l] for l in lanes], axis=0)
            dqt, dk, dv, delta = scores_backward(
                kv_ref[b, :, 0:HD], kv_ref[b, :, HD:], kt[...], bias[...], q, do
            )
            dq = dqt.T
            for i in range(4):
                total = (dq[i * BLK:(i + 1) * BLK] + dq_acc[rows, lanes[i]]) * SCALE
                dq_ref[rows, lanes[i]] = total.astype(BF)
            dkv_acc[:, 0:HD] += dk
            dkv_acc[:, HD:] += dv
            delta_s[b, pl.ds(g, 1), :] = delta
            return inner

        lax.fori_loop(0, 4, heads4, 0)
        factor = jnp.where(
            lax.broadcasted_iota(jnp.int32, (1, 2 * HD), 1) < HD, jnp.float32(SCALE), 1.0
        )
        dkv_ref[b] = (dkv_acc[...] * factor).astype(BF)
        down_ref[b] = dkv_acc[PICKS * BLK:, :] * factor
        return carry

    lax.fori_loop(0, QB, sel_block, 0)

    dck = (dc_acc[0] * SCALE).reshape(RANKS // 2, 8, HD)
    dcv = dc_acc[1].reshape(RANKS // 2, 8, HD)
    dcomp_ref[:, 0] = jnp.where(top_rows, dck, swap(dcv))
    dcomp_ref[:, 1] = jnp.where(top_rows, swap(dck), dcv)

    gate_t = jax.nn.sigmoid(nt(w_ref[0], x0) + nt(w_ref[1], x1))
    dz_ref[0:HEADS, :] = (delta_c[...] * (1.0 - gate_t[0:HEADS])).astype(BF)
    columns = []
    for b in range(QB):
        columns.append(
            jnp.concatenate([delta_s[b, :, i * BLK:(i + 1) * BLK] for i in range(4)], axis=0)
        )
    sel = jnp.concatenate(columns, axis=1)
    dz_ref[HEADS:, :] = (sel * (1.0 - gate_t[HEADS:])).astype(BF)


def return_kernel(
    dkv_ref, dcomp_ref, dz_ref,
    back_ref, csum_ref, dzother_ref,
    b_buf, b_sum, a_buf, kv_send, kv_recv, b_send, b_recv, a_send, a_recv, z_sems,
):
    me = lax.axis_index("ctx")
    hd = lax.axis_index("head")
    group = me // LOW
    low = me % LOW
    partner = {"head": 1 - hd}

    barrier = pltpu.get_barrier_semaphore()
    for g in range(OUTER):
        @pl.when(g > group)
        def _():
            signal(barrier, at_ctx(g * LOW + low))
    for p, j, r in REACH:
        @pl.when(me + r < RANKS)
        def _():
            signal(barrier, at_ctx(me + r))
    for a in range(LOW):
        @pl.when(a != low)
        def _():
            signal(barrier, at_ctx(group * LOW + a))
    signal(barrier, partner)
    owners = count([me >= r for _, _, r in REACH])
    pl.semaphore_wait(barrier, owners + group + (LOW - 1) + 1)

    def kv_copy(p, j, target):
        slot = p * PICKS + j
        return remote(
            dkv_ref.at[:, p, j], back_ref.at[slot], kv_send.at[slot], kv_recv.at[slot],
            at_ctx(target),
        )

    def b_copy(g, source):
        return remote(
            dcomp_ref.at[pl.ds(g * LOW, LOW)], b_buf.at[source], b_send.at[g], b_recv.at[source],
            at_ctx(g * LOW + low),
        )

    def a_copy(a, source):
        return remote(
            b_sum.at[a], a_buf.at[source], a_send.at[a], a_recv.at[source],
            at_ctx(group * LOW + a),
        )

    z_copy = remote(dz_ref, dzother_ref, z_sems.at[0], z_sems.at[1], partner)

    for g in range(OUTER):
        @pl.when(g < group)
        def _():
            b_copy(g, group).start()
    for p, j, r in REACH:
        @pl.when(me >= r)
        def _():
            kv_copy(p, j, me - r).start()
    z_copy.start()
    b_sum[...] = dcomp_ref[pl.ds(group * LOW, LOW)]
    for g in range(OUTER):
        @pl.when(g > group)
        def _():
            b_copy(g, g).wait_recv()
            b_sum[...] += b_buf[g]
    for a in range(LOW):
        @pl.when(a != low)
        def _():
            a_copy(a, low).start()
    a_buf[pl.ds(low, 1)] = b_sum[pl.ds(low, 1)]
    for a in range(LOW):
        @pl.when(a != low)
        def _():
            a_copy(a, a).wait_recv()
    csum_ref[...] = jnp.sum(a_buf[...], axis=0)
    z_copy.wait_recv()
    for p, j, r in REACH:
        @pl.when(me + r < RANKS)
        def _():
            kv_copy(p, j, me + r).wait_recv()
    for g in range(OUTER):
        @pl.when(g < group)
        def _():
            b_copy(g, group).wait_send()
    for p, j, r in REACH:
        @pl.when(me >= r)
        def _():
            kv_copy(p, j, me - r).wait_send()
    for a in range(LOW):
        @pl.when(a != low)
        def _():
            a_copy(a, low).wait_send()
    z_copy.wait_send()


def finish_kernel(
    sel_ref, back_ref, down_ref, csum_ref, dz_ref, dzother_ref, w_ref, wother_ref,
    dk_ref, dv_ref, dck_ref, dcv_ref, dx_ref, acc,
):
    me = lax.axis_index("ctx")
    hd = lax.axis_index("head")
    acc[...] = down_ref[...]
    for p, j, r in REACH:
        @pl.when(me + r < RANKS)
        def _():
            for i in range(2):
                local = sel_ref[((me + r) * QB + p + 2 * i) * PICKS + j] & (QB - 1)
                acc[local] += back_ref[p * PICKS + j, i].astype(F32)
    for b in range(QB):
        dk_ref[b * BLK:(b + 1) * BLK, :] = acc[b, :, 0:HD].astype(BF)
        dv_ref[b * BLK:(b + 1) * BLK, :] = acc[b, :, HD:].astype(BF)
    dck_ref[...] = csum_ref[0:4, :].astype(BF)
    dcv_ref[...] = csum_ref[4:8, :].astype(BF)
    mine = lax.dot_general(
        dz_ref[...], w_ref[hd], (((0,), (0,)), ((), ())), preferred_element_type=F32
    )
    other = lax.dot_general(
        dzother_ref[...], wother_ref[...], (((0,), (0,)), ((), ())), preferred_element_type=F32
    )
    dx_ref[...] = (mine + other).astype(BF)


VM = pl.BlockSpec(memory_space=pltpu.VMEM)
SM = pl.BlockSpec(memory_space=pltpu.SMEM)


def body(queries, keys, values, comp_keys, comp_values, selected, inputs, w_gate, d_out):
    tokens = queries.shape[0]
    width = inputs.shape[1]
    half = width // 2
    dma = lambda n: pltpu.SemaphoreType.DMA((n,))
    sel = selected.reshape(-1)
    w2 = w_gate.T.reshape(2 * HEADS, 2, half).transpose(1, 0, 2)
    slots = 2 * PICKS

    kv, comp, w_other = pl.pallas_call(
        fetch_kernel,
        name="fetch",
        out_shape=(
            jax.ShapeDtypeStruct((2, 2, PICKS + 1, BLK, 2 * HD), BF),
            jax.ShapeDtypeStruct((RANKS, 8, HD), F32),
            jax.ShapeDtypeStruct((2 * HEADS, half), BF),
        ),
        in_specs=[SM] + [VM] * 5,
        out_specs=(VM,) * 3,
        scratch_shapes=[
            pltpu.VMEM((slots, 2, BLK, 2 * HD), BF),
            dma(slots), dma(slots), dma(LOW), dma(LOW), dma(OUTER), dma(OUTER), dma(2),
        ],
        compiler_params=pltpu.CompilerParams(
            collective_id=0, has_side_effects=True, vmem_limit_bytes=16 * MIB
        ),
    )(sel, keys.reshape(QB, BLK, HD), values.reshape(QB, BLK, HD), comp_keys, comp_values, w2)

    keys_all = (PICKS + 1) * BLK
    dq, dkv, down, dcomp, dz = pl.pallas_call(
        local_kernel,
        name="local",
        out_shape=(
            jax.ShapeDtypeStruct(queries.shape, BF),
            jax.ShapeDtypeStruct((QB, keys_all, 2 * HD), BF),
            jax.ShapeDtypeStruct((QB, BLK, 2 * HD), F32),
            jax.ShapeDtypeStruct((RANKS // 2, 2, 8, HD), F32),
            jax.ShapeDtypeStruct((2 * HEADS, tokens), BF),
        ),
        in_specs=[VM] * 6,
        out_specs=(VM,) * 5,
        scratch_shapes=[
            pltpu.VMEM(queries.shape, BF),
            pltpu.VMEM(queries.shape, BF),
            pltpu.VMEM(queries.shape, F32),
            pltpu.VMEM((RANKS * QB, tokens), F32),
            pltpu.VMEM((2, keys_all, 4 * BLK), F32),
            pltpu.VMEM((RANKS * QB, HD), BF),
            pltpu.VMEM((RANKS * QB, HD), BF),
            pltpu.VMEM((HD, RANKS * QB), BF),
            pltpu.VMEM((HD, keys_all), BF),
            pltpu.VMEM((2, RANKS * QB, HD), F32),
            pltpu.VMEM((keys_all, 2 * HD), F32),
            pltpu.VMEM((HEADS, tokens), F32),
            pltpu.VMEM((QB, 4, 4 * BLK), F32),
        ],
        compiler_params=pltpu.CompilerParams(vmem_limit_bytes=48 * MIB),
    )(queries, d_out, inputs, w2, kv.reshape(QB, keys_all, 2 * HD), comp)

    back, csum, dz_other = pl.pallas_call(
        return_kernel,
        name="back",
        out_shape=(
            jax.ShapeDtypeStruct((slots, 2, BLK, 2 * HD), BF),
            jax.ShapeDtypeStruct((8, HD), F32),
            jax.ShapeDtypeStruct((2 * HEADS, tokens), BF),
        ),
        in_specs=[VM] * 3,
        out_specs=(VM,) * 3,
        scratch_shapes=[
            pltpu.VMEM((OUTER, LOW, 8, HD), F32),
            pltpu.VMEM((LOW, 8, HD), F32),
            pltpu.VMEM((LOW, 8, HD), F32),
            dma(slots), dma(slots), dma(OUTER), dma(OUTER), dma(LOW), dma(LOW), dma(2),
        ],
        compiler_params=pltpu.CompilerParams(
            collective_id=1, has_side_effects=True, vmem_limit_bytes=16 * MIB
        ),
    )(dkv.reshape(2, 2, PICKS + 1, BLK, 2 * HD), dcomp.reshape(RANKS, 8, HD), dz)

    dk, dv, dck, dcv, dx = pl.pallas_call(
        finish_kernel,
        name="finish",
        out_shape=(
            jax.ShapeDtypeStruct((tokens, HD), BF),
            jax.ShapeDtypeStruct((tokens, HD), BF),
            jax.ShapeDtypeStruct((QB, HD), BF),
            jax.ShapeDtypeStruct((QB, HD), BF),
            jax.ShapeDtypeStruct((tokens, half), BF),
        ),
        in_specs=[SM] + [VM] * 7,
        out_specs=(VM,) * 5,
        scratch_shapes=[pltpu.VMEM((QB, BLK, 2 * HD), F32)],
        compiler_params=pltpu.CompilerParams(vmem_limit_bytes=24 * MIB),
    )(sel, back, down, csum, dz, dz_other, w2, w_other)
    return dq, dk, dv, dck, dcv, dx


def solution(mesh):
    split = P("ctx", "head")
    in_specs = (split, split, split, split, split, P(), P("ctx", None), P(None, "head"), split)
    return jax.shard_map(body, mesh=mesh, in_specs=in_specs, out_specs=(split,) * 6, check_vma=False)
```

```python
import functools

import jax
import jax.numpy as jnp
from jax import lax
from jax.experimental import pallas as pl
from jax.experimental.pallas import tpu as pltpu
from jax.sharding import PartitionSpec as P

BLK = 64
PICKS = 15
HD = 128
QB = 4
RANKS = 128
HEADS = 16
LOW = 16
OUTER = RANKS // LOW
HALF = RANKS // 2
SCALE = HD ** -0.5
LOG2E = 1.4426950408889634
BF = jnp.bfloat16
F32 = jnp.float32
MIB = 1 << 20


def reach(parity, j):
    if parity == 0:
        return 1 + (j * (HALF - 1)) // (PICKS - 1)
    return HALF + 1 + (j * (HALF - 2)) // (PICKS - 1)


REACH = [(p, j, reach(p, j)) for p in range(2) for j in range(PICKS)]


def count(conditions):
    return sum(c.astype(jnp.int32) for c in conditions)


def at_ctx(index):
    return {"ctx": index}


def signal(sem, device):
    pl.semaphore_signal(sem, inc=1, device_id=device, device_id_type=pl.DeviceIdType.MESH)


def remote(src, dst, send_sem, recv_sem, device):
    return pltpu.make_async_remote_copy(
        src_ref=src,
        dst_ref=dst,
        send_sem=send_sem,
        recv_sem=recv_sem,
        device_id=device,
        device_id_type=pl.DeviceIdType.MESH,
    )


def nt(a, b):
    return lax.dot_general(a, b, (((1,), (1,)), ((), ())), preferred_element_type=F32)


def nn(a, b):
    return lax.dot_general(a, b, (((1,), (0,)), ((), ())), preferred_element_type=F32)


def scores_backward(k, v, kt, bias, q, do):
    s = nt(k, q) * (SCALE * LOG2E) + bias
    top = jnp.max(s, axis=0, keepdims=True)
    e = jnp.exp2(s - top)
    prob = e * (1.0 / jnp.sum(e, axis=0, keepdims=True))
    dp = nt(v, do)
    delta = jnp.sum(prob * dp, axis=0, keepdims=True)
    ds = (prob * (dp - delta)).astype(BF)
    dv = nn(prob.astype(BF), do)
    dk = nn(ds, q)
    dqt = nn(kt, ds)
    return dqt, dk, dv, delta


def reach_of(parity, j):
    near = 1 + (j * (HALF - 1)) // (PICKS - 1)
    far = HALF + 1 + (j * (HALF - 2)) // (PICKS - 1)
    return jnp.where(parity == 0, near, far)


def each(n, visit):
    def step(i, carry):
        visit(i)
        return carry

    lax.fori_loop(0, n, step, 0)


def attention_kernel(
    sel_ref, k_ref, v_ref, ck_ref, cv_ref, w_ref, q_hbm, do_hbm, x_hbm,
    dq_ref, back_ref, down_ref, csum_ref, dz_ref, dzother_ref, wother_ref,
    q_ref, do_ref, x_ref, out_buf, kv_ref, comp_ref, dkv_ref, dcomp_ref, b_buf, b_sum, a_buf,
    doc, dos, dq_acc, bias_c, bias_s, ck, cv, ckt, kt, dc_acc, dkv_acc, delta_c, delta_s,
    kv_send, kv_recv, g_send, g_recv, a_send, a_recv, b_send, b_recv,
    ra_send, ra_recv, rb_send, rb_recv, w_sems, z_sems, in_sems,
):
    me = lax.axis_index("ctx")
    hd = lax.axis_index("head")
    group = me // LOW
    low = me % LOW
    partner = {"head": 1 - hd}
    tokens = q_ref.shape[0]
    half = w_ref.shape[2]

    x_in = pltpu.make_async_copy(x_hbm, x_ref, in_sems.at[0])
    do_in = pltpu.make_async_copy(do_hbm, do_ref, in_sems.at[1])
    q_in = pltpu.make_async_copy(q_hbm, q_ref, in_sems.at[2])
    x_in.start()
    do_in.start()
    q_in.start()

    barrier = pltpu.get_barrier_semaphore()

    @functools.partial(each, LOW)
    def _(a):
        @pl.when(a != low)
        def _():
            signal(barrier, at_ctx(group * LOW + a))

    @functools.partial(each, OUTER)
    def _(g):
        @pl.when(g != group)
        def _():
            signal(barrier, at_ctx(g * LOW + low))

    @functools.partial(each, 2 * PICKS)
    def _(n):
        r = reach_of(n // PICKS, n % PICKS)

        @pl.when(me >= r)
        def _():
            signal(barrier, at_ctx(me - r))

        @pl.when(me + r < RANKS)
        def _():
            signal(barrier, at_ctx(me + r))

    signal(barrier, partner)

    comp_ref[pl.ds(me, 1), 0:4, :] = ck_ref[...].astype(F32)[None]
    comp_ref[pl.ds(me, 1), 4:8, :] = cv_ref[...].astype(F32)[None]

    @functools.partial(each, OUTER)
    def _(g):
        @pl.when(g > group)
        def _():
            comp_ref[pl.ds(g * LOW, LOW)] = jnp.zeros((LOW, 8, HD), F32)

    for b in range(QB):
        @functools.partial(each, PICKS)
        def _(j):
            r = reach_of(b % 2, j)
            asker = jnp.minimum(me + r, RANKS - 1)
            local = sel_ref[(asker * QB + b) * PICKS + j] & (QB - 1)
            out_buf[b, j, :, 0:HD] = k_ref[local]
            out_buf[b, j, :, HD:] = v_ref[local]

            @pl.when(me < r)
            def _():
                kv_ref[b, j] = jnp.zeros((BLK, 2 * HD), BF)

        kv_ref[b, PICKS, :, 0:HD] = k_ref[b]
        kv_ref[b, PICKS, :, HD:] = v_ref[b]

    peers = count(
        [me + r < RANKS for _, _, r in REACH] + [me >= r for _, _, r in REACH]
    )
    pl.semaphore_wait(barrier, peers + (LOW - 1) + (OUTER - 1) + 1)

    def a_copy(a, slot):
        return remote(
            comp_ref.at[slot], comp_ref.at[slot], a_send.at[a], a_recv.at[slot % LOW],
            at_ctx(group * LOW + a),
        )

    def b_copy(g, source):
        rows = pl.ds(source * LOW, LOW)
        return remote(
            comp_ref.at[rows], comp_ref.at[rows], b_send.at[g], b_recv.at[source],
            at_ctx(g * LOW + low),
        )

    def kv_copy(b, j, target):
        return remote(
            out_buf.at[b, j], kv_ref.at[b, j], kv_send.at[b, j], kv_recv.at[b, j], at_ctx(target)
        )

    def grad_copy(b, j, target):
        return remote(
            dkv_ref.at[b, j], back_ref.at[b, j], g_send.at[b, j], g_recv.at[b, j], at_ctx(target)
        )

    def rb_copy(g, source):
        return remote(
            dcomp_ref.at[pl.ds(g * LOW, LOW)], b_buf.at[source], rb_send.at[g], rb_recv.at[source],
            at_ctx(g * LOW + low),
        )

    def ra_copy(a, source):
        return remote(
            b_sum.at[a], a_buf.at[source], ra_send.at[a], ra_recv.at[source],
            at_ctx(group * LOW + a),
        )

    w_copy = remote(w_ref.at[1 - hd], wother_ref, w_sems.at[0], w_sems.at[1], partner)
    z_copy = remote(dz_ref, dzother_ref, z_sems.at[0], z_sems.at[1], partner)

    def others_low(visit):
        @functools.partial(each, LOW)
        def _(a):
            @pl.when(a != low)
            def _():
                visit(a)

    def outer_where(test, visit):
        @functools.partial(each, OUTER)
        def _(g):
            @pl.when(test(g))
            def _():
                visit(g)

    def askers(b, visit):
        @functools.partial(each, PICKS)
        def _(j):
            r = reach_of(b % 2, j)

            @pl.when(me + r < RANKS)
            def _():
                visit(j, me + r)

    def owners(b, visit):
        @functools.partial(each, PICKS)
        def _(j):
            r = reach_of(b % 2, j)

            @pl.when(me >= r)
            def _():
                visit(j, me - r)

    others_low(lambda a: a_copy(a, me).start())
    askers(0, lambda j, t: kv_copy(0, j, t).start())
    others_low(lambda a: a_copy(a, group * LOW + a).wait_recv())
    outer_where(lambda g: g > group, lambda g: b_copy(g, group).start())
    for b in range(1, QB):
        askers(b, lambda j, t: kv_copy(b, j, t).start())
    w_copy.start()

    row = lax.broadcasted_iota(jnp.int32, (RANKS * QB, tokens), 0)
    col = lax.broadcasted_iota(jnp.int32, (RANKS * QB, tokens), 1)
    bias_c[...] = jnp.where(row <= me * QB + col // BLK, 0.0, -jnp.inf)
    srow = lax.broadcasted_iota(jnp.int32, (BLK, 4 * BLK), 0)
    scol = lax.broadcasted_iota(jnp.int32, (BLK, 4 * BLK), 1) % BLK
    own_bias = jnp.where(srow <= scol, 0.0, -jnp.inf)
    for p, j, r in REACH:
        bias_s[p, j * BLK:(j + 1) * BLK, :] = jnp.full(
            (BLK, 4 * BLK), jnp.where(me >= r, 0.0, -jnp.inf), F32
        )
    for p in range(2):
        bias_s[p, PICKS * BLK:, :] = own_bias
    x_in.wait()
    do_in.wait()
    gate = jax.nn.sigmoid(nt(x_ref[:, 0:half], w_ref[0]) + nt(x_ref[:, half:], w_ref[1]))
    for h in range(HEADS):
        slab = do_ref[:, h * HD:(h + 1) * HD].astype(F32)
        doc[:, h * HD:(h + 1) * HD] = (gate[:, h:h + 1] * slab).astype(BF)
        dos[:, h * HD:(h + 1) * HD] = (gate[:, HEADS + h:HEADS + h + 1] * slab).astype(BF)
    q_in.wait()

    outer_where(lambda g: g < group, lambda g: b_copy(g, g).wait_recv())
    pairs = comp_ref[...].reshape(RANKS // 2, 2, 8, HD)
    even, odd = pairs[:, 0], pairs[:, 1]
    top_rows = lax.broadcasted_iota(jnp.int32, (RANKS // 2, 8, HD), 1) < 4
    swap = lambda z: pltpu.roll(z, 4, 1)
    keys_c = jnp.where(top_rows, even, swap(odd)).reshape(RANKS * 4, HD)
    vals_c = jnp.where(top_rows, swap(even), odd).reshape(RANKS * 4, HD)
    ck[...] = keys_c.astype(BF)
    cv[...] = vals_c.astype(BF)
    ckt[...] = keys_c.T.astype(BF)
    dc_acc[...] = jnp.zeros_like(dc_acc)

    @functools.partial(each, HEADS)
    def _(h):
        lanes = pl.ds(pl.multiple_of(h * HD, HD), HD)
        dqt, dk, dv, delta = scores_backward(
            ck[...], cv[...], ckt[...], bias_c[...], q_ref[:, lanes], doc[:, lanes]
        )
        dq_acc[:, lanes] = dqt.T
        dc_acc[0] += dk
        dc_acc[1] += dv
        delta_c[pl.ds(h, 1), :] = delta

    dck = (dc_acc[0] * SCALE).reshape(RANKS // 2, 8, HD)
    dcv = dc_acc[1].reshape(RANKS // 2, 8, HD)
    dcomp_ref[...] = jnp.stack(
        [jnp.where(top_rows, dck, swap(dcv)), jnp.where(top_rows, swap(dck), dcv)], axis=1
    ).reshape(RANKS, 8, HD)
    outer_where(lambda g: g < group, lambda g: rb_copy(g, group).start())

    @functools.partial(each, QB)
    def _(b):
        owners(b, lambda j, t: kv_copy(b, j, t).wait_recv())
        rows = pl.ds(pl.multiple_of(b * BLK, BLK), BLK)
        keys_all = (PICKS + 1) * BLK
        kt[...] = kv_ref[b, :, :, 0:HD].reshape(keys_all, HD).astype(F32).T.astype(BF)
        dkv_acc[...] = jnp.zeros_like(dkv_acc)
        bias = bias_s.at[b % 2]

        @functools.partial(each, 4)
        def _(g):
            lanes = [pl.ds(pl.multiple_of((g + 4 * i) * HD, HD), HD) for i in range(4)]
            q = jnp.concatenate([q_ref[rows, l] for l in lanes], axis=0)
            do = jnp.concatenate([dos[rows, l] for l in lanes], axis=0)
            dqt, dk, dv, delta = scores_backward(
                kv_ref[b, :, :, 0:HD].reshape(keys_all, HD),
                kv_ref[b, :, :, HD:].reshape(keys_all, HD),
                kt[...], bias[...], q, do,
            )
            dq = dqt.T
            for i in range(4):
                total = (dq[i * BLK:(i + 1) * BLK] + dq_acc[rows, lanes[i]]) * SCALE
                dq_ref[rows, lanes[i]] = total.astype(BF)
            dkv_acc[:, 0:HD] += dk
            dkv_acc[:, HD:] += dv
            delta_s[b, pl.ds(g, 1), :] = delta

        factor = jnp.where(
            lax.broadcasted_iota(jnp.int32, (1, 2 * HD), 1) < HD, jnp.float32(SCALE), 1.0
        )
        total = dkv_acc[...] * factor
        dkv_ref[b] = total[0:PICKS * BLK].astype(BF).reshape(PICKS, BLK, 2 * HD)
        down_ref[b] = total[PICKS * BLK:]
        owners(b, lambda j, t: grad_copy(b, j, t).start())

    gate_t = jax.nn.sigmoid(nt(w_ref[0], x_ref[:, 0:half]) + nt(w_ref[1], x_ref[:, half:]))
    dz_ref[0:HEADS, :] = (delta_c[...] * (1.0 - gate_t[0:HEADS])).astype(BF)
    columns = []
    for b in range(QB):
        columns.append(
            jnp.concatenate([delta_s[b, :, i * BLK:(i + 1) * BLK] for i in range(4)], axis=0)
        )
    sel = jnp.concatenate(columns, axis=1)
    dz_ref[HEADS:, :] = (sel * (1.0 - gate_t[HEADS:])).astype(BF)
    z_copy.start()

    b_sum[...] = dcomp_ref[pl.ds(group * LOW, LOW)]

    def add_outer(g):
        rb_copy(g, g).wait_recv()
        b_sum[...] += b_buf[g]

    outer_where(lambda g: g > group, add_outer)
    others_low(lambda a: ra_copy(a, low).start())
    a_buf[pl.ds(low, 1)] = b_sum[pl.ds(low, 1)]
    others_low(lambda a: ra_copy(a, a).wait_recv())
    csum_ref[...] = jnp.sum(a_buf[...], axis=0)

    w_copy.wait_recv()
    z_copy.wait_recv()
    for b in range(QB):
        askers(b, lambda j, t: grad_copy(b, j, t).wait_recv())
    for b in range(QB):
        askers(b, lambda j, t: kv_copy(b, j, t).wait_send())
        owners(b, lambda j, t: grad_copy(b, j, t).wait_send())
    others_low(lambda a: a_copy(a, me).wait_send())
    outer_where(lambda g: g > group, lambda g: b_copy(g, group).wait_send())
    outer_where(lambda g: g < group, lambda g: rb_copy(g, group).wait_send())
    others_low(lambda a: ra_copy(a, low).wait_send())
    w_copy.wait_send()
    z_copy.wait_send()


def finish_kernel(
    sel_ref, back_ref, down_ref, csum_ref, dz_ref, dzother_ref, w_ref, wother_ref,
    dk_ref, dv_ref, dck_ref, dcv_ref, dx_ref, acc,
):
    me = lax.axis_index("ctx")
    hd = lax.axis_index("head")
    acc[...] = down_ref[...]
    for p, j, r in REACH:
        @pl.when(me + r < RANKS)
        def _():
            for i in range(2):
                local = sel_ref[((me + r) * QB + p + 2 * i) * PICKS + j] & (QB - 1)
                acc[local] += back_ref[p + 2 * i, j].astype(F32)
    for b in range(QB):
        dk_ref[b * BLK:(b + 1) * BLK, :] = acc[b, :, 0:HD].astype(BF)
        dv_ref[b * BLK:(b + 1) * BLK, :] = acc[b, :, HD:].astype(BF)
    dck_ref[...] = csum_ref[0:4, :].astype(BF)
    dcv_ref[...] = csum_ref[4:8, :].astype(BF)
    mine = lax.dot_general(
        dz_ref[...], w_ref[hd], (((0,), (0,)), ((), ())), preferred_element_type=F32
    )
    other = lax.dot_general(
        dzother_ref[...], wother_ref[...], (((0,), (0,)), ((), ())), preferred_element_type=F32
    )
    dx_ref[...] = (mine + other).astype(BF)


VM = pl.BlockSpec(memory_space=pltpu.VMEM)
SM = pl.BlockSpec(memory_space=pltpu.SMEM)


def body(queries, keys, values, comp_keys, comp_values, selected, inputs, w_gate, d_out):
    tokens = queries.shape[0]
    width = inputs.shape[1]
    half = width // 2
    dma = lambda *n: pltpu.SemaphoreType.DMA(n)
    vm = lambda *shape: pltpu.VMEM(shape, BF)
    vf = lambda *shape: pltpu.VMEM(shape, F32)
    sel = selected.reshape(-1)
    w2 = w_gate.T.reshape(2 * HEADS, 2, half).transpose(1, 0, 2)
    keys_all = (PICKS + 1) * BLK
    blocks = (QB, BLK, HD)

    dq, back, down, csum, dz, dz_other, w_other = pl.pallas_call(
        attention_kernel,
        name="attention",
        out_shape=(
            jax.ShapeDtypeStruct(queries.shape, BF),
            jax.ShapeDtypeStruct((QB, PICKS, BLK, 2 * HD), BF),
            jax.ShapeDtypeStruct((QB, BLK, 2 * HD), F32),
            jax.ShapeDtypeStruct((8, HD), F32),
            jax.ShapeDtypeStruct((2 * HEADS, tokens), BF),
            jax.ShapeDtypeStruct((2 * HEADS, tokens), BF),
            jax.ShapeDtypeStruct((2 * HEADS, half), BF),
        ),
        in_specs=[SM] + [VM] * 5 + [pl.BlockSpec(memory_space=pl.ANY)] * 3,
        out_specs=(VM,) * 7,
        scratch_shapes=[
            vm(*queries.shape), vm(*d_out.shape), vm(*inputs.shape),
            vm(QB, PICKS, BLK, 2 * HD), vm(QB, PICKS + 1, BLK, 2 * HD), vf(RANKS, 8, HD),
            vm(QB, PICKS, BLK, 2 * HD), vf(RANKS, 8, HD),
            vf(OUTER, LOW, 8, HD), vf(LOW, 8, HD), vf(LOW, 8, HD),
            vm(*queries.shape), vm(*queries.shape), vf(*queries.shape),
            vf(RANKS * QB, tokens), vf(2, keys_all, 4 * BLK),
            vm(RANKS * QB, HD), vm(RANKS * QB, HD), vm(HD, RANKS * QB), vm(HD, keys_all),
            vf(2, RANKS * QB, HD), vf(keys_all, 2 * HD), vf(HEADS, tokens), vf(QB, 4, 4 * BLK),
            dma(QB, PICKS), dma(QB, PICKS), dma(QB, PICKS), dma(QB, PICKS),
            dma(LOW), dma(LOW), dma(OUTER), dma(OUTER),
            dma(LOW), dma(LOW), dma(OUTER), dma(OUTER), dma(2), dma(2), dma(3),
        ],
        compiler_params=pltpu.CompilerParams(
            collective_id=0, has_side_effects=True, vmem_limit_bytes=48 * MIB
        ),
    )(
        sel, keys.reshape(blocks), values.reshape(blocks), comp_keys, comp_values, w2,
        queries, d_out, inputs,
    )

    dk, dv, dck, dcv, dx = pl.pallas_call(
        finish_kernel,
        name="finish",
        out_shape=(
            jax.ShapeDtypeStruct((tokens, HD), BF),
            jax.ShapeDtypeStruct((tokens, HD), BF),
            jax.ShapeDtypeStruct((QB, HD), BF),
            jax.ShapeDtypeStruct((QB, HD), BF),
            jax.ShapeDtypeStruct((tokens, half), BF),
        ),
        in_specs=[SM] + [VM] * 7,
        out_specs=(VM,) * 5,
        scratch_shapes=[pltpu.VMEM((QB, BLK, 2 * HD), F32)],
        compiler_params=pltpu.CompilerParams(vmem_limit_bytes=24 * MIB),
    )(sel, back, down, csum, dz, dz_other, w2, w_other)
    return dq, dk, dv, dck, dcv, dx


def solution(mesh):
    split = P("ctx", "head")
    in_specs = (split, split, split, split, split, P(), P("ctx", None), P(None, "head"), split)
    return jax.shard_map(body, mesh=mesh, in_specs=in_specs, out_specs=(split,) * 6, check_vma=False)
```

```python
import functools

import jax
import jax.numpy as jnp
from jax import lax
from jax.experimental import pallas as pl
from jax.experimental.pallas import tpu as pltpu
from jax.sharding import PartitionSpec as P

BLK = 64
PICKS = 15
HD = 128
QB = 4
RANKS = 128
HEADS = 16
LOW = 16
OUTER = RANKS // LOW
HALF = RANKS // 2
PLANE = 32
RELAYS = PICKS // 2
SCALE = HD ** -0.5
LOG2E = 1.4426950408889634
BF = jnp.bfloat16
F32 = jnp.float32
MIB = 1 << 20


def reach(parity, j):
    if parity == 0:
        return 1 + (j * (HALF - 1)) // (PICKS - 1)
    return HALF + 1 + (j * (HALF - 2)) // (PICKS - 1)


REACH = [(p, j, reach(p, j)) for p in range(2) for j in range(PICKS)]


def count(conditions):
    return sum(c.astype(jnp.int32) for c in conditions)


def at_ctx(index):
    return {"ctx": index}


def signal(sem, device):
    pl.semaphore_signal(sem, inc=1, device_id=device, device_id_type=pl.DeviceIdType.MESH)


def remote(src, dst, send_sem, recv_sem, device):
    return pltpu.make_async_remote_copy(
        src_ref=src,
        dst_ref=dst,
        send_sem=send_sem,
        recv_sem=recv_sem,
        device_id=device,
        device_id_type=pl.DeviceIdType.MESH,
    )


def nt(a, b):
    return lax.dot_general(a, b, (((1,), (1,)), ((), ())), preferred_element_type=F32)


def nn(a, b):
    return lax.dot_general(a, b, (((1,), (0,)), ((), ())), preferred_element_type=F32)


def scores_backward(k, v, kt, bias, q, do):
    s = nt(k, q) * (SCALE * LOG2E) + bias
    top = jnp.max(s, axis=0, keepdims=True)
    e = jnp.exp2(s - top)
    prob = e * (1.0 / jnp.sum(e, axis=0, keepdims=True))
    dp = nt(v, do)
    delta = jnp.sum(prob * dp, axis=0, keepdims=True)
    ds = (prob * (dp - delta)).astype(BF)
    dv = nn(prob.astype(BF), do)
    dk = nn(ds, q)
    dqt = nn(kt, ds)
    return dqt, dk, dv, delta


def reach_of(parity, j):
    near = 1 + (j * (HALF - 1)) // (PICKS - 1)
    far = HALF + 1 + (j * (HALF - 2)) // (PICKS - 1)
    return jnp.where(parity == 0, near, far)


def relayed(j, source, target):
    odd = (j % 2 == 1) & (source // PLANE != target // PLANE)
    return odd & (source % PLANE != target % PLANE)


def stop(j, source, target):
    relay = target // PLANE * PLANE + source % PLANE
    return jnp.where(relayed(j, source, target), relay, target)


def each(n, visit):
    def step(i, carry):
        visit(i)
        return carry

    lax.fori_loop(0, n, step, 0)


def attention_kernel(
    sel_ref, ck_ref, cv_ref, k_hbm, v_hbm, w_hbm, q_hbm, do_hbm, x_hbm,
    dq_ref, down_ref, csum_ref, dz_ref, dzother_ref, wother_ref,
    k_ref, v_ref, w_ref, q_ref, do_ref, x_ref, back_ref, relay_f, relay_b, out_buf, kv_ref, comp_ref, dkv_ref, dcomp_ref, b_buf, b_sum, a_buf,
    doc, dos, dq_acc, bias_c, bias_s, ck, cv, ckt, kt, dc_acc, dkv_acc, delta_c, delta_s,
    kv_send, kv_recv, g_send, g_recv, f_send, f_recv, h_send, h_recv, a_send, a_recv, b_send, b_recv,
    ra_send, ra_recv, rb_send, rb_recv, w_sems, z_sems, in_sems,
):
    me = lax.axis_index("ctx")
    hd = lax.axis_index("head")
    group = me // LOW
    low = me % LOW
    partner = {"head": 1 - hd}
    tokens = q_ref.shape[0]
    half = w_ref.shape[1] // 2
    place = me % PLANE

    k_in = pltpu.make_async_copy(k_hbm, k_ref, in_sems.at[3])
    v_in = pltpu.make_async_copy(v_hbm, v_ref, in_sems.at[4])
    w_in = pltpu.make_async_copy(w_hbm, w_ref, in_sems.at[5])
    k_in.start()
    v_in.start()
    w_in.start()
    x_in = pltpu.make_async_copy(x_hbm, x_ref, in_sems.at[0])
    do_in = pltpu.make_async_copy(do_hbm, do_ref, in_sems.at[1])
    q_in = pltpu.make_async_copy(q_hbm, q_ref, in_sems.at[2])
    x_in.start()
    do_in.start()
    q_in.start()

    barrier = pltpu.get_barrier_semaphore()

    @functools.partial(each, PLANE)
    def _(a):
        @pl.when(a != place)
        def _():
            signal(barrier, at_ctx(me - place + a))

    @functools.partial(each, OUTER)
    def _(g):
        @pl.when(g != group)
        def _():
            signal(barrier, at_ctx(g * LOW + low))

    @functools.partial(each, 2 * PICKS)
    def _(n):
        r = reach_of(n // PICKS, n % PICKS)

        @pl.when(me >= r)
        def _():
            signal(barrier, at_ctx(me - r))

        @pl.when(me + r < RANKS)
        def _():
            signal(barrier, at_ctx(me + r))

    signal(barrier, partner)

    comp_ref[pl.ds(me, 1), 0:4, :] = ck_ref[...].astype(F32)[None]
    comp_ref[pl.ds(me, 1), 4:8, :] = cv_ref[...].astype(F32)[None]

    @functools.partial(each, OUTER)
    def _(g):
        @pl.when(g > group)
        def _():
            comp_ref[pl.ds(g * LOW, LOW)] = jnp.zeros((LOW, 8, HD), F32)

    k_in.wait()
    v_in.wait()
    for b in range(QB):
        @functools.partial(each, PICKS)
        def _(j):
            r = reach_of(b % 2, j)
            asker = jnp.minimum(me + r, RANKS - 1)
            local = sel_ref[j, asker * QB + b] & (QB - 1)
            out_buf[b, j, :, 0:HD] = k_ref[local]
            out_buf[b, j, :, HD:] = v_ref[local]

            @pl.when(me < r)
            def _():
                kv_ref[b, j] = jnp.zeros((BLK, 2 * HD), BF)

        kv_ref[b, PICKS, :, 0:HD] = k_ref[b]
        kv_ref[b, PICKS, :, HD:] = v_ref[b]

    peers = count(
        [me + r < RANKS for _, _, r in REACH] + [me >= r for _, _, r in REACH]
    )
    pl.semaphore_wait(barrier, peers + (PLANE - 1) + (OUTER - 1) + 1)

    def a_copy(a, slot):
        return remote(
            comp_ref.at[slot], comp_ref.at[slot], a_send.at[a], a_recv.at[slot % LOW],
            at_ctx(group * LOW + a),
        )

    def b_copy(g, source):
        rows = pl.ds(source * LOW, LOW)
        return remote(
            comp_ref.at[rows], comp_ref.at[rows], b_send.at[g], b_recv.at[source],
            at_ctx(g * LOW + low),
        )

    def relay_copy(b, j, target):
        return remote(
            out_buf.at[b, j], relay_f.at[b, j // 2], kv_send.at[b, j], f_recv.at[b, j // 2],
            at_ctx(target),
        )

    def forward_copy(b, i, target):
        return remote(
            relay_f.at[b, i], kv_ref.at[b, 2 * i + 1], f_send.at[b, i],
            kv_recv.at[b, 2 * i + 1], at_ctx(target),
        )

    def grad_relay_copy(b, j, target):
        return remote(
            dkv_ref.at[b, j], relay_b.at[b, j // 2], g_send.at[b, j], h_recv.at[b, j // 2],
            at_ctx(target),
        )

    def grad_forward_copy(b, i, target):
        return remote(
            relay_b.at[b, i], back_ref.at[b, 2 * i + 1], h_send.at[b, i],
            g_recv.at[b, 2 * i + 1], at_ctx(target),
        )

    def kv_copy(b, j, target):
        return remote(
            out_buf.at[b, j], kv_ref.at[b, j], kv_send.at[b, j], kv_recv.at[b, j], at_ctx(target)
        )

    def grad_copy(b, j, target):
        return remote(
            dkv_ref.at[b, j], back_ref.at[b, j], g_send.at[b, j], g_recv.at[b, j], at_ctx(target)
        )

    def rb_copy(g, source):
        return remote(
            dcomp_ref.at[pl.ds(g * LOW, LOW)], b_buf.at[source], rb_send.at[g], rb_recv.at[source],
            at_ctx(g * LOW + low),
        )

    def ra_copy(a, source):
        return remote(
            b_sum.at[a], a_buf.at[source], ra_send.at[a], ra_recv.at[source],
            at_ctx(group * LOW + a),
        )

    theirs = pl.ds(pl.multiple_of((1 - hd) * half, HD), half)
    w_copy = remote(w_ref.at[:, theirs], wother_ref, w_sems.at[0], w_sems.at[1], partner)
    z_copy = remote(dz_ref, dzother_ref, z_sems.at[0], z_sems.at[1], partner)

    def others_low(visit):
        @functools.partial(each, LOW)
        def _(a):
            @pl.when(a != low)
            def _():
                visit(a)

    def outer_where(test, visit):
        @functools.partial(each, OUTER)
        def _(g):
            @pl.when(test(g))
            def _():
                visit(g)

    def askers(b, visit):
        @functools.partial(each, PICKS)
        def _(j):
            r = reach_of(b % 2, j)

            @pl.when(me + r < RANKS)
            def _():
                visit(j, me + r)

    def owners(b, visit):
        @functools.partial(each, PICKS)
        def _(j):
            r = reach_of(b % 2, j)

            @pl.when(me >= r)
            def _():
                visit(j, me - r)

    def fetch_forwards(b, i, visit):
        r = reach_of(b % 2, 2 * i + 1)
        planes = (place + r) // PLANE
        source = me - PLANE * planes
        target = source + r

        @pl.when((planes > 0) & (source >= 0) & (target != me))
        def _():
            visit(target)

    def grad_forwards(b, i, visit):
        r = reach_of(b % 2, 2 * i + 1)
        planes = (r - place + PLANE - 1) // PLANE
        source = me + PLANE * planes
        target = source - r

        @pl.when((r > place) & (source < RANKS) & (target != me))
        def _():
            visit(target)

    def send_relayed(b):
        def visit(j, t):
            @pl.when(relayed(j, me, t))
            def _():
                relay_copy(b, j, stop(j, me, t)).start()

        askers(b, visit)

    def send_direct(b):
        def visit(j, t):
            @pl.when(jnp.logical_not(relayed(j, me, t)))
            def _():
                kv_copy(b, j, t).start()

        askers(b, visit)

    others_low(lambda a: a_copy(a, me).start())
    for b in range(QB):
        send_relayed(b)
    others_low(lambda a: a_copy(a, group * LOW + a).wait_recv())
    outer_where(lambda g: g > group, lambda g: b_copy(g, group).start())
    for b in range(QB):
        send_direct(b)
    w_in.wait()
    w_copy.start()

    row = lax.broadcasted_iota(jnp.int32, (RANKS * QB, tokens), 0)
    col = lax.broadcasted_iota(jnp.int32, (RANKS * QB, tokens), 1)
    bias_c[...] = jnp.where(row <= me * QB + col // BLK, 0.0, -jnp.inf)
    srow = lax.broadcasted_iota(jnp.int32, (BLK, 4 * BLK), 0)
    scol = lax.broadcasted_iota(jnp.int32, (BLK, 4 * BLK), 1) % BLK
    own_bias = jnp.where(srow <= scol, 0.0, -jnp.inf)
    for p, j, r in REACH:
        bias_s[p, j * BLK:(j + 1) * BLK, :] = jnp.full(
            (BLK, 4 * BLK), jnp.where(me >= r, 0.0, -jnp.inf), F32
        )
    for p in range(2):
        bias_s[p, PICKS * BLK:, :] = own_bias
    x_in.wait()
    do_in.wait()
    gate = jax.nn.sigmoid(nt(x_ref[...], w_ref[...]))
    for h in range(HEADS):
        slab = do_ref[:, h * HD:(h + 1) * HD].astype(F32)
        doc[:, h * HD:(h + 1) * HD] = (gate[:, h:h + 1] * slab).astype(BF)
        dos[:, h * HD:(h + 1) * HD] = (gate[:, HEADS + h:HEADS + h + 1] * slab).astype(BF)
    q_in.wait()

    outer_where(lambda g: g < group, lambda g: b_copy(g, g).wait_recv())
    pairs = comp_ref[...].reshape(RANKS // 2, 2, 8, HD)
    even, odd = pairs[:, 0], pairs[:, 1]
    top_rows = lax.broadcasted_iota(jnp.int32, (RANKS // 2, 8, HD), 1) < 4
    swap = lambda z: pltpu.roll(z, 4, 1)
    keys_c = jnp.where(top_rows, even, swap(odd)).reshape(RANKS * 4, HD)
    vals_c = jnp.where(top_rows, swap(even), odd).reshape(RANKS * 4, HD)
    ck[...] = keys_c.astype(BF)
    cv[...] = vals_c.astype(BF)
    ckt[...] = keys_c.T.astype(BF)
    dc_acc[...] = jnp.zeros_like(dc_acc)

    @functools.partial(each, HEADS)
    def _(h):
        @pl.when(h < QB * RELAYS // 2)
        def _():
            for i in range(2):
                n = 2 * h + i
                b, entry = n // RELAYS, n % RELAYS

                def pass_on(target):
                    relay_copy(b, 2 * entry + 1, target).wait_recv()
                    forward_copy(b, entry, target).start()

                fetch_forwards(b, entry, pass_on)

        lanes = pl.ds(pl.multiple_of(h * HD, HD), HD)
        dqt, dk, dv, delta = scores_backward(
            ck[...], cv[...], ckt[...], bias_c[...], q_ref[:, lanes], doc[:, lanes]
        )
        dq_acc[:, lanes] = dqt.T
        dc_acc[0] += dk
        dc_acc[1] += dv
        delta_c[pl.ds(h, 1), :] = delta

    dck = (dc_acc[0] * SCALE).reshape(RANKS // 2, 8, HD)
    dcv = dc_acc[1].reshape(RANKS // 2, 8, HD)
    dcomp_ref[...] = jnp.stack(
        [jnp.where(top_rows, dck, swap(dcv)), jnp.where(top_rows, swap(dck), dcv)], axis=1
    ).reshape(RANKS, 8, HD)
    outer_where(lambda g: g < group, lambda g: rb_copy(g, group).start())

    @functools.partial(each, QB)
    def _(b):
        owners(b, lambda j, t: kv_copy(b, j, t).wait_recv())
        rows = pl.ds(pl.multiple_of(b * BLK, BLK), BLK)
        keys_all = (PICKS + 1) * BLK
        kt[...] = kv_ref[b, :, :, 0:HD].reshape(keys_all, HD).astype(F32).T.astype(BF)
        dkv_acc[...] = jnp.zeros_like(dkv_acc)
        bias = bias_s.at[b % 2]

        @functools.partial(each, 4)
        def _(g):
            lanes = [pl.ds(pl.multiple_of((g + 4 * i) * HD, HD), HD) for i in range(4)]
            q = jnp.concatenate([q_ref[rows, l] for l in lanes], axis=0)
            do = jnp.concatenate([dos[rows, l] for l in lanes], axis=0)
            dqt, dk, dv, delta = scores_backward(
                kv_ref[b, :, :, 0:HD].reshape(keys_all, HD),
                kv_ref[b, :, :, HD:].reshape(keys_all, HD),
                kt[...], bias[...], q, do,
            )
            dq = dqt.T
            for i in range(4):
                total = (dq[i * BLK:(i + 1) * BLK] + dq_acc[rows, lanes[i]]) * SCALE
                dq_ref[rows, lanes[i]] = total.astype(BF)
            dkv_acc[:, 0:HD] += dk
            dkv_acc[:, HD:] += dv
            delta_s[b, pl.ds(g, 1), :] = delta

        factor = jnp.where(
            lax.broadcasted_iota(jnp.int32, (1, 2 * HD), 1) < HD, jnp.float32(SCALE), 1.0
        )
        total = dkv_acc[...] * factor
        dkv_ref[b] = total[0:PICKS * BLK].astype(BF).reshape(PICKS, BLK, 2 * HD)
        down_ref[b] = total[PICKS * BLK:]

        def send_grad(j, t):
            hop = relayed(j, me, t) & (b < QB - 1)

            @pl.when(hop)
            def _():
                grad_relay_copy(b, j, stop(j, me, t)).start()

            @pl.when(jnp.logical_not(hop))
            def _():
                grad_copy(b, j, t).start()

        owners(b, send_grad)

        @pl.when(b > 0)
        def _():
            @functools.partial(each, RELAYS)
            def _(i):
                def pass_on(target):
                    grad_relay_copy(b - 1, 2 * i + 1, target).wait_recv()
                    grad_forward_copy(b - 1, i, target).start()

                grad_forwards(b - 1, i, pass_on)

    gate_t = jax.nn.sigmoid(nt(w_ref[...], x_ref[...]))
    dz_ref[0:HEADS, :] = (delta_c[...] * (1.0 - gate_t[0:HEADS])).astype(BF)
    columns = []
    for b in range(QB):
        columns.append(
            jnp.concatenate([delta_s[b, :, i * BLK:(i + 1) * BLK] for i in range(4)], axis=0)
        )
    sel = jnp.concatenate(columns, axis=1)
    dz_ref[HEADS:, :] = (sel * (1.0 - gate_t[HEADS:])).astype(BF)
    z_copy.start()

    b_sum[...] = dcomp_ref[pl.ds(group * LOW, LOW)]

    def add_outer(g):
        rb_copy(g, g).wait_recv()
        b_sum[...] += b_buf[g]

    outer_where(lambda g: g > group, add_outer)
    others_low(lambda a: ra_copy(a, low).start())
    a_buf[pl.ds(low, 1)] = b_sum[pl.ds(low, 1)]

    def add_arrived(b):
        def visit(j, t):
            grad_copy(b, j, t).wait_recv()
            local = sel_ref[j, t * QB + b] & (QB - 1)
            term = back_ref[b, j].astype(F32)
            for c in range(QB):
                down_ref[c] += jnp.where(local == c, term, 0.0)

        askers(b, visit)

    for b in range(QB):
        add_arrived(b)
    others_low(lambda a: ra_copy(a, a).wait_recv())
    csum_ref[...] = jnp.sum(a_buf[...], axis=0)
    w_copy.wait_recv()
    z_copy.wait_recv()
    for b in range(QB):
        askers(b, lambda j, t: kv_copy(b, j, t).wait_send())
        owners(b, lambda j, t: grad_copy(b, j, t).wait_send())

        @functools.partial(each, RELAYS)
        def _(i):
            fetch_forwards(b, i, lambda t: forward_copy(b, i, t).wait_send())
            if b < QB - 1:
                grad_forwards(b, i, lambda t: grad_forward_copy(b, i, t).wait_send())

    others_low(lambda a: a_copy(a, me).wait_send())
    outer_where(lambda g: g > group, lambda g: b_copy(g, group).wait_send())
    outer_where(lambda g: g < group, lambda g: rb_copy(g, group).wait_send())
    others_low(lambda a: ra_copy(a, low).wait_send())
    w_copy.wait_send()
    z_copy.wait_send()


def finish_kernel(
    down_ref, csum_ref, dz_ref, dzother_ref, w_ref, wother_ref, dk_ref, dv_ref, dck_ref, dcv_ref, dx_ref
):
    hd = lax.axis_index("head")
    half = wother_ref.shape[1]
    mine = pl.ds(pl.multiple_of(hd * half, HD), half)
    for b in range(QB):
        dk_ref[b * BLK:(b + 1) * BLK, :] = down_ref[b, :, 0:HD].astype(BF)
        dv_ref[b * BLK:(b + 1) * BLK, :] = down_ref[b, :, HD:].astype(BF)
    dck_ref[...] = csum_ref[0:4, :].astype(BF)
    dcv_ref[...] = csum_ref[4:8, :].astype(BF)
    tn = lambda a, c: lax.dot_general(a, c, (((0,), (0,)), ((), ())), preferred_element_type=F32)
    dx_ref[...] = (tn(dz_ref[...], w_ref[:, mine]) + tn(dzother_ref[...], wother_ref[...])).astype(BF)


VM = pl.BlockSpec(memory_space=pltpu.VMEM)
SM = pl.BlockSpec(memory_space=pltpu.SMEM)


def body(queries, keys, values, comp_keys, comp_values, selected, inputs, w_gate, d_out):
    tokens = queries.shape[0]
    width = inputs.shape[1]
    half = width // 2
    dma = lambda *n: pltpu.SemaphoreType.DMA(n)
    vm = lambda *shape: pltpu.VMEM(shape, BF)
    vf = lambda *shape: pltpu.VMEM(shape, F32)
    sel = selected.T
    wt = w_gate.T
    keys_all = (PICKS + 1) * BLK
    blocks = (QB, BLK, HD)

    dq, down, csum, dz, dz_other, w_other = pl.pallas_call(
        attention_kernel,
        name="attention",
        out_shape=(
            jax.ShapeDtypeStruct(queries.shape, BF),
            jax.ShapeDtypeStruct((QB, BLK, 2 * HD), F32),
            jax.ShapeDtypeStruct((8, HD), F32),
            jax.ShapeDtypeStruct((2 * HEADS, tokens), BF),
            jax.ShapeDtypeStruct((2 * HEADS, tokens), BF),
            jax.ShapeDtypeStruct((2 * HEADS, half), BF),
        ),
        in_specs=[SM] + [VM] * 2 + [pl.BlockSpec(memory_space=pl.ANY)] * 6,
        out_specs=(VM,) * 6,
        scratch_shapes=[
            vm(*blocks), vm(*blocks), vm(*wt.shape),
            vm(*queries.shape), vm(*d_out.shape), vm(*inputs.shape),
            vm(QB, PICKS, BLK, 2 * HD), vm(QB, RELAYS, BLK, 2 * HD), vm(QB, RELAYS, BLK, 2 * HD),
            vm(QB, PICKS, BLK, 2 * HD), vm(QB, PICKS + 1, BLK, 2 * HD), vf(RANKS, 8, HD),
            vm(QB, PICKS, BLK, 2 * HD), vf(RANKS, 8, HD),
            vf(OUTER, LOW, 8, HD), vf(LOW, 8, HD), vf(LOW, 8, HD),
            vm(*queries.shape), vm(*queries.shape), vf(*queries.shape),
            vf(RANKS * QB, tokens), vf(2, keys_all, 4 * BLK),
            vm(RANKS * QB, HD), vm(RANKS * QB, HD), vm(HD, RANKS * QB), vm(HD, keys_all),
            vf(2, RANKS * QB, HD), vf(keys_all, 2 * HD), vf(HEADS, tokens), vf(QB, 4, 4 * BLK),
            dma(QB, PICKS), dma(QB, PICKS), dma(QB, PICKS), dma(QB, PICKS),
            dma(QB, RELAYS), dma(QB, RELAYS), dma(QB, RELAYS), dma(QB, RELAYS),
            dma(LOW), dma(LOW), dma(OUTER), dma(OUTER),
            dma(LOW), dma(LOW), dma(OUTER), dma(OUTER), dma(2), dma(2), dma(6),
        ],
        compiler_params=pltpu.CompilerParams(
            collective_id=0, has_side_effects=True, vmem_limit_bytes=60 * MIB
        ),
    )(
        sel, comp_keys, comp_values, keys.reshape(blocks), values.reshape(blocks), wt,
        queries, d_out, inputs,
    )

    dk, dv, dck, dcv, dx = pl.pallas_call(
        finish_kernel,
        name="finish",
        out_shape=(
            jax.ShapeDtypeStruct((tokens, HD), BF),
            jax.ShapeDtypeStruct((tokens, HD), BF),
            jax.ShapeDtypeStruct((QB, HD), BF),
            jax.ShapeDtypeStruct((QB, HD), BF),
            jax.ShapeDtypeStruct((tokens, half), BF),
        ),
        in_specs=[VM] * 6,
        out_specs=(VM,) * 5,
        compiler_params=pltpu.CompilerParams(vmem_limit_bytes=24 * MIB),
    )(down, csum, dz, dz_other, wt, w_other)
    return dq, dk, dv, dck, dcv, dx


def solution(mesh):
    split = P("ctx", "head")
    in_specs = (split, split, split, split, split, P(), P("ctx", None), P(None, "head"), split)
    return jax.shard_map(body, mesh=mesh, in_specs=in_specs, out_specs=(split,) * 6, check_vma=False)
```

```python
import functools

import jax
import jax.numpy as jnp
from jax import lax
from jax.experimental import pallas as pl
from jax.experimental.pallas import tpu as pltpu
from jax.sharding import PartitionSpec as P

BLK = 64
PICKS = 15
HD = 128
QB = 4
RANKS = 128
HEADS = 16
LOW = 32
OUTER = RANKS // LOW
HALF = RANKS // 2
PLANE = 32
RELAYS = PICKS // 2
SCALE = HD ** -0.5
LOG2E = 1.4426950408889634
BF = jnp.bfloat16
F32 = jnp.float32
MIB = 1 << 20


def reach(parity, j):
    if parity == 0:
        return 1 + (j * (HALF - 1)) // (PICKS - 1)
    return HALF + 1 + (j * (HALF - 2)) // (PICKS - 1)


REACH = [(p, j, reach(p, j)) for p in range(2) for j in range(PICKS)]


def count(conditions):
    return sum(c.astype(jnp.int32) for c in conditions)


def at_ctx(index):
    return {"ctx": index}


def signal(sem, device):
    pl.semaphore_signal(sem, inc=1, device_id=device, device_id_type=pl.DeviceIdType.MESH)


def remote(src, dst, send_sem, recv_sem, device):
    return pltpu.make_async_remote_copy(
        src_ref=src,
        dst_ref=dst,
        send_sem=send_sem,
        recv_sem=recv_sem,
        device_id=device,
        device_id_type=pl.DeviceIdType.MESH,
    )


def nt(a, b):
    return lax.dot_general(a, b, (((1,), (1,)), ((), ())), preferred_element_type=F32)


def nn(a, b):
    return lax.dot_general(a, b, (((1,), (0,)), ((), ())), preferred_element_type=F32)


def scores_backward(k, v, kt, bias, q, do):
    s = nt(k, q) * (SCALE * LOG2E) + bias
    top = jnp.max(s, axis=0, keepdims=True)
    e = jnp.exp2(s - top)
    prob = e * (1.0 / jnp.sum(e, axis=0, keepdims=True))
    dp = nt(v, do)
    delta = jnp.sum(prob * dp, axis=0, keepdims=True)
    ds = (prob * (dp - delta)).astype(BF)
    dv = nn(prob.astype(BF), do)
    dk = nn(ds, q)
    dqt = nn(kt, ds)
    return dqt, dk, dv, delta


def reach_of(parity, j):
    return jnp.where(parity == 0, 1 + ((j * 9) >> 1), HALF + 1 + ((j * 31 * 9363) >> 16))


for _p, _j, _r in REACH:
    assert _r == (1 + ((_j * 9) >> 1) if _p == 0 else HALF + 1 + ((_j * 31 * 9363) >> 16))


def crosses(source, target):
    return ((source >> 5) != (target >> 5)) & ((source & 31) != (target & 31))


def stop(source, target):
    return (target & ~31) | (source & 31)


def each(n, visit):
    def step(i, carry):
        visit(i)
        return carry

    lax.fori_loop(0, n, step, 0)


def attention_kernel(
    sel_ref, ck_ref, cv_ref, k_hbm, v_hbm, w_hbm, q_hbm, do_hbm, x_hbm,
    dq_hbm, down_ref, csum_ref, dz_ref, dzother_ref, wother_ref,
    dq_ref, k_ref, v_ref, w_ref, q_ref, do_ref, x_ref, back_ref, relay_f, relay_b, out_buf, kv_ref, comp_ref, dkv_ref, dcomp_ref, b_buf, b_sum, a_buf,
    doc, dos, dq_acc, bias_c, bias_s, ck, cv, ckt, kt, dc_acc, dkv_acc, delta_c, delta_s,
    kv_send, kv_recv, g_send, g_recv, f_send, f_recv, h_send, h_recv, a_send, a_recv, b_send, b_recv,
    ra_send, ra_recv, rb_send, rb_recv, w_sems, z_sems, in_sems, dq_sems,
):
    me = lax.axis_index("ctx")
    hd = lax.axis_index("head")
    group = me >> 5
    low = me & 31
    partner = {"head": 1 - hd}
    tokens = q_ref.shape[0]
    half = w_ref.shape[1] // 2
    place = me & 31

    k_in = pltpu.make_async_copy(k_hbm, k_ref, in_sems.at[3])
    v_in = pltpu.make_async_copy(v_hbm, v_ref, in_sems.at[4])
    w_in = pltpu.make_async_copy(w_hbm, w_ref, in_sems.at[5])
    k_in.start()
    v_in.start()
    w_in.start()
    x_in = pltpu.make_async_copy(x_hbm, x_ref, in_sems.at[0])
    do_in = pltpu.make_async_copy(do_hbm, do_ref, in_sems.at[1])
    q_in = pltpu.make_async_copy(q_hbm, q_ref, in_sems.at[2])
    x_in.start()
    do_in.start()
    q_in.start()

    barrier = pltpu.get_barrier_semaphore()

    @functools.partial(each, PLANE)
    def _(a):
        @pl.when(a != place)
        def _():
            signal(barrier, at_ctx(me - place + a))

    @functools.partial(each, OUTER)
    def _(g):
        @pl.when(g != group)
        def _():
            signal(barrier, at_ctx(g * LOW + low))

    for p, j, r in REACH:
        @pl.when(me >= r)
        def _():
            signal(barrier, at_ctx(me - r))

        @pl.when(me + r < RANKS)
        def _():
            signal(barrier, at_ctx(me + r))

    signal(barrier, partner)

    own = jnp.concatenate([ck_ref[...].astype(F32), cv_ref[...].astype(F32)], axis=0)
    comp_ref[pl.ds(me, 1)] = own.astype(BF)[None]

    @functools.partial(each, OUTER)
    def _(g):
        @pl.when(g > group)
        def _():
            comp_ref[pl.ds(g * LOW, LOW)] = jnp.zeros((LOW, 8, HD), BF)

    k_in.wait()
    v_in.wait()
    for p, j, r in REACH:
        asker = jnp.minimum(me + r, RANKS - 1)
        for i in range(2):
            local = sel_ref[j, asker * QB + (p + 2 * i)] & (QB - 1)
            out_buf[p, j, i, :, 0:HD] = k_ref[local]
            out_buf[p, j, i, :, HD:] = v_ref[local]

        @pl.when(me < r)
        def _():
            kv_ref[:, p, j] = jnp.zeros((2, BLK, 2 * HD), BF)

    for b in range(QB):
        kv_ref[b // 2, b % 2, PICKS, :, 0:HD] = k_ref[b]
        kv_ref[b // 2, b % 2, PICKS, :, HD:] = v_ref[b]

    peers = count(
        [me + r < RANKS for _, _, r in REACH] + [me >= r for _, _, r in REACH]
    )
    pl.semaphore_wait(barrier, peers + (PLANE - 1) + (OUTER - 1) + 1)

    def a_copy(a, slot):
        return remote(
            comp_ref.at[slot], comp_ref.at[slot], a_send.at[a], a_recv.at[slot & 31],
            at_ctx(group * LOW + a),
        )

    def b_copy(g, source):
        rows = pl.ds(source * LOW, LOW)
        return remote(
            comp_ref.at[rows], comp_ref.at[rows], b_send.at[g], b_recv.at[source],
            at_ctx(g * LOW + low),
        )

    def relay_copy(p, i, target):
        return remote(
            out_buf.at[p, 2 * i + 1], relay_f.at[p, i], kv_send.at[p, 2 * i + 1], f_recv.at[p, i],
            at_ctx(target),
        )

    def forward_copy(p, i, target):
        return remote(
            relay_f.at[p, i], kv_ref.at[:, p, 2 * i + 1], f_send.at[p, i],
            kv_recv.at[p, 2 * i + 1], at_ctx(target),
        )

    def grad_relay_copy(b, j, target):
        return remote(
            dkv_ref.at[b, j], relay_b.at[b, j >> 1], g_send.at[b, j], h_recv.at[b, j >> 1],
            at_ctx(target),
        )

    def grad_forward_copy(b, i, target):
        return remote(
            relay_b.at[b, i], back_ref.at[b, 2 * i + 1], h_send.at[b, i],
            g_recv.at[b, 2 * i + 1], at_ctx(target),
        )

    def kv_copy(p, j, target):
        return remote(
            out_buf.at[p, j], kv_ref.at[:, p, j], kv_send.at[p, j], kv_recv.at[p, j], at_ctx(target)
        )

    def grad_copy(b, j, target):
        return remote(
            dkv_ref.at[b, j], back_ref.at[b, j], g_send.at[b, j], g_recv.at[b, j], at_ctx(target)
        )

    def rb_copy(g, source):
        return remote(
            dcomp_ref.at[pl.ds(g * LOW, LOW)], b_buf.at[source], rb_send.at[g], rb_recv.at[source],
            at_ctx(g * LOW + low),
        )

    def ra_copy(a, source):
        return remote(
            b_sum.at[a], a_buf.at[source], ra_send.at[a], ra_recv.at[source],
            at_ctx(group * LOW + a),
        )

    theirs = pl.ds(pl.multiple_of((1 - hd) * half, HD), half)
    w_copy = remote(w_ref.at[:, theirs], wother_ref, w_sems.at[0], w_sems.at[1], partner)
    z_copy = remote(dz_ref, dzother_ref, z_sems.at[0], z_sems.at[1], partner)

    def others_low(visit):
        @functools.partial(each, LOW)
        def _(a):
            @pl.when(a != low)
            def _():
                visit(a)

    def outer_where(test, visit):
        @functools.partial(each, OUTER)
        def _(g):
            @pl.when(test(g))
            def _():
                visit(g)

    def owners(b, visit):
        for j in range(PICKS):
            r = jnp.where((b & 1) == 0, reach(0, j), reach(1, j))

            @pl.when(me >= r)
            def _():
                visit(j, me - r)

    def fetch_forwards(p, i, visit):
        r = reach_of(p, 2 * i + 1)
        planes = (place + r) >> 5
        source = me - PLANE * planes
        target = source + r

        @pl.when((planes > 0) & (source >= 0) & (target != me))
        def _():
            visit(target)

    def grad_forwards(b, i, visit):
        r = reach_of(b & 1, 2 * i + 1)
        planes = (r - place + PLANE - 1) >> 5
        source = me + PLANE * planes
        target = source - r

        @pl.when((r > place) & (source < RANKS) & (target != me))
        def _():
            visit(target)

    def send_relayed(q):
        for p, j, r in REACH:
            if p == q and j % 2 == 1 and r % PLANE != 0:
                @pl.when((me + r < RANKS) & crosses(me, me + r))
                def _():
                    relay_copy(p, j // 2, stop(me, me + r)).start()

    def send_direct(q):
        for p, j, r in REACH[q * PICKS:(q + 1) * PICKS]:
            inside = me + r < RANKS
            if j % 2 == 1 and r % PLANE != 0:
                inside = inside & jnp.logical_not(crosses(me, me + r))

            @pl.when(inside)
            def _():
                kv_copy(p, j, me + r).start()

    others_low(lambda a: a_copy(a, me).start())
    send_relayed(0)
    others_low(lambda a: a_copy(a, group * LOW + a).wait_recv())
    outer_where(lambda g: g > group, lambda g: b_copy(g, group).start())
    send_direct(0)
    send_relayed(1)
    w_in.wait()
    w_copy.start()

    row = lax.broadcasted_iota(jnp.int32, (RANKS * QB, tokens), 0)
    col = lax.broadcasted_iota(jnp.int32, (RANKS * QB, tokens), 1)
    bias_c[...] = jnp.where(row <= me * QB + (col >> 6), 0.0, -jnp.inf)
    srow = lax.broadcasted_iota(jnp.int32, (BLK, 4 * BLK), 0)
    scol = lax.broadcasted_iota(jnp.int32, (BLK, 4 * BLK), 1) % BLK
    own_bias = jnp.where(srow <= scol, 0.0, -jnp.inf)
    for p, j, r in REACH:
        bias_s[p, j * BLK:(j + 1) * BLK, :] = jnp.full(
            (BLK, 4 * BLK), jnp.where(me >= r, 0.0, -jnp.inf), F32
        )
    for p in range(2):
        bias_s[p, PICKS * BLK:, :] = own_bias
    x_in.wait()
    do_in.wait()
    gate = jax.nn.sigmoid(nt(x_ref[...], w_ref[...]))
    for h in range(HEADS):
        slab = do_ref[:, h * HD:(h + 1) * HD].astype(F32)
        doc[:, h * HD:(h + 1) * HD] = (gate[:, h:h + 1] * slab).astype(BF)
        dos[:, h * HD:(h + 1) * HD] = (gate[:, HEADS + h:HEADS + h + 1] * slab).astype(BF)
    q_in.wait()

    outer_where(lambda g: g < group, lambda g: b_copy(g, g).wait_recv())
    pairs = comp_ref[...].astype(F32).reshape(RANKS // 2, 2, 8, HD)
    even, odd = pairs[:, 0], pairs[:, 1]
    top_rows = lax.broadcasted_iota(jnp.int32, (RANKS // 2, 8, HD), 1) < 4
    swap = lambda z: pltpu.roll(z, 4, 1)
    keys_c = jnp.where(top_rows, even, swap(odd)).reshape(RANKS * 4, HD)
    vals_c = jnp.where(top_rows, swap(even), odd).reshape(RANKS * 4, HD)
    ck[...] = keys_c.astype(BF)
    cv[...] = vals_c.astype(BF)
    ckt[...] = keys_c.T.astype(BF)
    dc_acc[...] = jnp.zeros_like(dc_acc)

    @functools.partial(each, HEADS)
    def _(h):
        @pl.when(h < 2 * RELAYS)
        def _():
            p = (h >= RELAYS).astype(jnp.int32)
            i = h - RELAYS * p

            def pass_on(target):
                relay_copy(p, i, target).wait_recv()
                forward_copy(p, i, target).start()

            fetch_forwards(p, i, pass_on)

        @pl.when(h == 8)
        def _():
            send_direct(1)

        lanes = pl.ds(pl.multiple_of(h * HD, HD), HD)
        dqt, dk, dv, delta = scores_backward(
            ck[...], cv[...], ckt[...], bias_c[...], q_ref[:, lanes], doc[:, lanes]
        )
        dq_acc[:, lanes] = dqt.T
        dc_acc[0] += dk
        dc_acc[1] += dv
        delta_c[pl.ds(h, 1), :] = delta

    dck = (dc_acc[0] * SCALE).reshape(RANKS // 2, 8, HD)
    dcv = dc_acc[1].reshape(RANKS // 2, 8, HD)
    dcomp_ref[...] = jnp.stack(
        [jnp.where(top_rows, dck, swap(dcv)), jnp.where(top_rows, swap(dck), dcv)], axis=1
    ).reshape(RANKS, 8, HD)
    outer_where(lambda g: g < group, lambda g: rb_copy(g, group).start())

    def dq_out(b):
        rows = pl.ds(pl.multiple_of(b * BLK, BLK), BLK)
        return pltpu.make_async_copy(dq_ref.at[rows], dq_hbm.at[rows], dq_sems.at[b])

    @functools.partial(each, QB)
    def _(b):
        @pl.when(b < 2)
        def _():
            owners(b, lambda j, t: kv_copy(b, j, t).wait_recv())

        @pl.when(b == 2)
        def _():
            b_sum[...] = dcomp_ref[pl.ds(group * LOW, LOW)]

            def add_outer(g):
                rb_copy(g, g).wait_recv()
                b_sum[...] += b_buf[g]

            outer_where(lambda g: g > group, add_outer)
            others_low(lambda a: ra_copy(a, low).start())
            a_buf[pl.ds(low, 1)] = b_sum[pl.ds(low, 1)]

        rows = pl.ds(pl.multiple_of(b * BLK, BLK), BLK)
        keys_all = (PICKS + 1) * BLK
        kt[...] = kv_ref[b >> 1, b & 1, :, :, 0:HD].reshape(keys_all, HD).astype(F32).T.astype(BF)
        dkv_acc[...] = jnp.zeros_like(dkv_acc)
        bias = bias_s.at[b & 1]

        @functools.partial(each, 4)
        def _(g):
            lanes = [pl.ds(pl.multiple_of((g + 4 * i) * HD, HD), HD) for i in range(4)]
            q = jnp.concatenate([q_ref[rows, l] for l in lanes], axis=0)
            do = jnp.concatenate([dos[rows, l] for l in lanes], axis=0)
            dqt, dk, dv, delta = scores_backward(
                kv_ref[b >> 1, b & 1, :, :, 0:HD].reshape(keys_all, HD),
                kv_ref[b >> 1, b & 1, :, :, HD:].reshape(keys_all, HD),
                kt[...], bias[...], q, do,
            )
            dq = dqt.T
            for i in range(4):
                total = (dq[i * BLK:(i + 1) * BLK] + dq_acc[rows, lanes[i]]) * SCALE
                dq_ref[rows, lanes[i]] = total.astype(BF)
            dkv_acc[:, 0:HD] += dk
            dkv_acc[:, HD:] += dv
            delta_s[b, pl.ds(g, 1), :] = delta

        factor = jnp.where(
            lax.broadcasted_iota(jnp.int32, (1, 2 * HD), 1) < HD, jnp.float32(SCALE), 1.0
        )
        total = dkv_acc[...] * factor
        dkv_ref[b] = total[0:PICKS * BLK].astype(BF).reshape(PICKS, BLK, 2 * HD)
        down_ref[b] = total[PICKS * BLK:]

        def send_grad(j, t):
            if j % 2 == 0:
                grad_copy(b, j, t).start()
            else:
                hop = crosses(me, t) & (b < QB - 1)

                @pl.when(hop)
                def _():
                    grad_relay_copy(b, j, stop(me, t)).start()

                @pl.when(jnp.logical_not(hop))
                def _():
                    grad_copy(b, j, t).start()

        owners(b, send_grad)
        dq_out(b).start()

        @pl.when(b > 0)
        def _():
            @functools.partial(each, RELAYS)
            def _(i):
                def pass_on(target):
                    grad_relay_copy(b - 1, 2 * i + 1, target).wait_recv()
                    grad_forward_copy(b - 1, i, target).start()

                grad_forwards(b - 1, i, pass_on)

    gate_t = jax.nn.sigmoid(nt(w_ref[...], x_ref[...]))
    dz_ref[0:HEADS, :] = (delta_c[...] * (1.0 - gate_t[0:HEADS])).astype(BF)
    columns = []
    for b in range(QB):
        columns.append(
            jnp.concatenate([delta_s[b, :, i * BLK:(i + 1) * BLK] for i in range(4)], axis=0)
        )
    sel = jnp.concatenate(columns, axis=1)
    dz_ref[HEADS:, :] = (sel * (1.0 - gate_t[HEADS:])).astype(BF)
    z_copy.start()

    for b in range(QB):
        @functools.partial(each, PICKS)
        def _(j):
            t = me + reach_of(b & 1, j)

            @pl.when(t < RANKS)
            def _():
                grad_copy(b, j, t).wait_recv()
                local = sel_ref[j, t * QB + b] & (QB - 1)
                term = back_ref[b, j].astype(F32)
                for c in range(QB):
                    down_ref[c] += jnp.where(local == c, term, 0.0)

    others_low(lambda a: ra_copy(a, a).wait_recv())
    csum_ref[...] = jnp.sum(a_buf[...], axis=0)
    w_copy.wait_recv()
    z_copy.wait_recv()
    each(QB, lambda b: dq_out(b).wait())
    for p, j, r in REACH:
        @pl.when(me + r < RANKS)
        def _():
            kv_copy(p, j, me + r).wait_send()

    for p in range(2):
        @functools.partial(each, RELAYS)
        def _(i):
            fetch_forwards(p, i, lambda t: forward_copy(p, i, t).wait_send())

    @functools.partial(each, QB)
    def _(b):
        owners(b, lambda j, t: grad_copy(b, j, t).wait_send())

    @functools.partial(each, QB - 1)
    def _(b):
        @functools.partial(each, RELAYS)
        def _(i):
            grad_forwards(b, i, lambda t: grad_forward_copy(b, i, t).wait_send())

    others_low(lambda a: a_copy(a, me).wait_send())
    outer_where(lambda g: g > group, lambda g: b_copy(g, group).wait_send())
    outer_where(lambda g: g < group, lambda g: rb_copy(g, group).wait_send())
    others_low(lambda a: ra_copy(a, low).wait_send())
    w_copy.wait_send()
    z_copy.wait_send()


def finish_kernel(
    dq_hbm, down_hbm, csum_hbm, dz_hbm, dzother_hbm, w_hbm, wother_hbm,
    dqo_ref, dk_ref, dv_ref, dck_ref, dcv_ref, dx_ref,
    down_ref, csum_ref, dz_ref, dzother_ref, w_ref, wother_ref, sems,
):
    hd = lax.axis_index("head")
    half = wother_ref.shape[1]
    mine = pl.ds(pl.multiple_of(hd * half, HD), half)
    pairs = [
        (dz_hbm, dz_ref), (dzother_hbm, dzother_ref), (w_hbm.at[:, mine], w_ref),
        (wother_hbm, wother_ref), (down_hbm, down_ref), (csum_hbm, csum_ref), (dq_hbm, dqo_ref),
    ]
    copies = [pltpu.make_async_copy(a, c, sems.at[i]) for i, (a, c) in enumerate(pairs)]
    copies[-1].start()
    for copy in copies[:-1]:
        copy.start()
    for copy in copies[:-1]:
        copy.wait()
    for b in range(QB):
        dk_ref[b * BLK:(b + 1) * BLK, :] = down_ref[b, :, 0:HD].astype(BF)
        dv_ref[b * BLK:(b + 1) * BLK, :] = down_ref[b, :, HD:].astype(BF)
    dck_ref[...] = csum_ref[0:4, :].astype(BF)
    dcv_ref[...] = csum_ref[4:8, :].astype(BF)
    tn = lambda a, c: lax.dot_general(a, c, (((0,), (0,)), ((), ())), preferred_element_type=F32)
    dx_ref[...] = (tn(dz_ref[...], w_ref[...]) + tn(dzother_ref[...], wother_ref[...])).astype(BF)
    copies[-1].wait()


VM = pl.BlockSpec(memory_space=pltpu.VMEM)
SM = pl.BlockSpec(memory_space=pltpu.SMEM)


def body(queries, keys, values, comp_keys, comp_values, selected, inputs, w_gate, d_out):
    tokens = queries.shape[0]
    width = inputs.shape[1]
    half = width // 2
    dma = lambda *n: pltpu.SemaphoreType.DMA(n)
    vm = lambda *shape: pltpu.VMEM(shape, BF)
    vf = lambda *shape: pltpu.VMEM(shape, F32)
    sel = selected.T
    wt = w_gate.T
    keys_all = (PICKS + 1) * BLK
    blocks = (QB, BLK, HD)

    dq, down, csum, dz, dz_other, w_other = pl.pallas_call(
        attention_kernel,
        name="attention",
        out_shape=(
            jax.ShapeDtypeStruct(queries.shape, BF),
            jax.ShapeDtypeStruct((QB, BLK, 2 * HD), F32),
            jax.ShapeDtypeStruct((8, HD), F32),
            jax.ShapeDtypeStruct((2 * HEADS, tokens), BF),
            jax.ShapeDtypeStruct((2 * HEADS, tokens), BF),
            jax.ShapeDtypeStruct((2 * HEADS, half), BF),
        ),
        in_specs=[SM] + [VM] * 2 + [pl.BlockSpec(memory_space=pl.ANY)] * 6,
        out_specs=(pl.BlockSpec(memory_space=pl.ANY),) + (VM,) * 5,
        scratch_shapes=[
            vm(*queries.shape),
            vm(*blocks), vm(*blocks), vm(*wt.shape),
            vm(*queries.shape), vm(*d_out.shape), vm(*inputs.shape),
            vm(QB, PICKS, BLK, 2 * HD),
            vm(2, RELAYS, 2, BLK, 2 * HD), vm(QB - 1, RELAYS, BLK, 2 * HD),
            vm(2, PICKS, 2, BLK, 2 * HD), vm(2, 2, PICKS + 1, BLK, 2 * HD), vm(RANKS, 8, HD),
            vm(QB, PICKS, BLK, 2 * HD), vf(RANKS, 8, HD),
            vf(OUTER, LOW, 8, HD), vf(LOW, 8, HD), vf(LOW, 8, HD),
            vm(*queries.shape), vm(*queries.shape), vf(*queries.shape),
            vf(RANKS * QB, tokens), vf(2, keys_all, 4 * BLK),
            vm(RANKS * QB, HD), vm(RANKS * QB, HD), vm(HD, RANKS * QB), vm(HD, keys_all),
            vf(2, RANKS * QB, HD), vf(keys_all, 2 * HD), vf(HEADS, tokens), vf(QB, 4, 4 * BLK),
            dma(2, PICKS), dma(2, PICKS), dma(QB, PICKS), dma(QB, PICKS),
            dma(2, RELAYS), dma(2, RELAYS), dma(QB - 1, RELAYS), dma(QB - 1, RELAYS),
            dma(LOW), dma(LOW), dma(OUTER), dma(OUTER),
            dma(LOW), dma(LOW), dma(OUTER), dma(OUTER), dma(2), dma(2), dma(6), dma(QB),
        ],
        compiler_params=pltpu.CompilerParams(
            collective_id=0, has_side_effects=True, vmem_limit_bytes=60 * MIB
        ),
    )(
        sel, comp_keys, comp_values, keys.reshape(blocks), values.reshape(blocks), wt,
        queries, d_out, inputs,
    )

    any_space = pl.BlockSpec(memory_space=pl.ANY)
    return pl.pallas_call(
        finish_kernel,
        name="finish",
        out_shape=(
            jax.ShapeDtypeStruct(queries.shape, BF),
            jax.ShapeDtypeStruct((tokens, HD), BF),
            jax.ShapeDtypeStruct((tokens, HD), BF),
            jax.ShapeDtypeStruct((QB, HD), BF),
            jax.ShapeDtypeStruct((QB, HD), BF),
            jax.ShapeDtypeStruct((tokens, half), BF),
        ),
        in_specs=[any_space] * 7,
        out_specs=(VM,) * 6,
        scratch_shapes=[
            vf(QB, BLK, 2 * HD), vf(8, HD), vm(2 * HEADS, tokens), vm(2 * HEADS, tokens),
            vm(2 * HEADS, half), vm(2 * HEADS, half), dma(7),
        ],
        compiler_params=pltpu.CompilerParams(vmem_limit_bytes=60 * MIB),
    )(dq, down, csum, dz, dz_other, wt, w_other)


def solution(mesh):
    split = P("ctx", "head")
    in_specs = (split, split, split, split, split, P(), P("ctx", None), P(None, "head"), split)
    return jax.shard_map(body, mesh=mesh, in_specs=in_specs, out_specs=(split,) * 6, check_vma=False)
```

```python
import functools

import jax
import jax.numpy as jnp
from jax import lax
from jax.experimental import pallas as pl
from jax.experimental.pallas import tpu as pltpu
from jax.sharding import PartitionSpec as P

BLK = 64
PICKS = 15
HD = 128
QB = 4
RANKS = 128
HEADS = 16
LOW = 32
OUTER = RANKS // LOW
HALF = RANKS // 2
PLANE = 32
RELAYS = PICKS // 2
SCALE = HD ** -0.5
LOG2E = 1.4426950408889634
BF = jnp.bfloat16
F32 = jnp.float32
MIB = 1 << 20


def reach(parity, j):
    if parity == 0:
        return 1 + (j * (HALF - 1)) // (PICKS - 1)
    return HALF + 1 + (j * (HALF - 2)) // (PICKS - 1)


REACH = [(p, j, reach(p, j)) for p in range(2) for j in range(PICKS)]


def count(conditions):
    return sum(c.astype(jnp.int32) for c in conditions)


def at_ctx(index):
    return {"ctx": index}


def signal(sem, device):
    pl.semaphore_signal(sem, inc=1, device_id=device, device_id_type=pl.DeviceIdType.MESH)


def remote(src, dst, send_sem, recv_sem, device):
    return pltpu.make_async_remote_copy(
        src_ref=src,
        dst_ref=dst,
        send_sem=send_sem,
        recv_sem=recv_sem,
        device_id=device,
        device_id_type=pl.DeviceIdType.MESH,
    )


def nt(a, b):
    return lax.dot_general(a, b, (((1,), (1,)), ((), ())), preferred_element_type=F32)


def nn(a, b):
    return lax.dot_general(a, b, (((1,), (0,)), ((), ())), preferred_element_type=F32)


def scores_backward(k, v, kt, bias, pairs):
    s = [nt(k, q) * (SCALE * LOG2E) + bias for q, _ in pairs]
    dp = [nt(v, do) for _, do in pairs]
    outs = []
    for i, (q, do) in enumerate(pairs):
        top = jnp.max(s[i], axis=0, keepdims=True)
        e = jnp.exp2(s[i] - top)
        prob = e * (1.0 / jnp.sum(e, axis=0, keepdims=True))
        delta = jnp.sum(prob * dp[i], axis=0, keepdims=True)
        ds = (prob * (dp[i] - delta)).astype(BF)
        dv = nn(prob.astype(BF), do)
        dk = nn(ds, q)
        dqt = nn(kt, ds)
        outs.append((dqt, dk, dv, delta))
    return outs


def reach_of(parity, j):
    return jnp.where(parity == 0, 1 + ((j * 9) >> 1), HALF + 1 + ((j * 31 * 9363) >> 16))


for _p, _j, _r in REACH:
    assert _r == (1 + ((_j * 9) >> 1) if _p == 0 else HALF + 1 + ((_j * 31 * 9363) >> 16))


def crosses(source, target):
    return ((source >> 5) != (target >> 5)) & ((source & 31) != (target & 31))


def stop(source, target):
    return (target & ~31) | (source & 31)


def each(n, visit):
    def step(i, carry):
        visit(i)
        return carry

    lax.fori_loop(0, n, step, 0)


def attention_kernel(
    sel_ref, ck_ref, cv_ref, k_hbm, v_hbm, w_hbm, q_hbm, do_hbm, x_hbm,
    dq_hbm, down_ref, csum_ref, dz_ref, dzother_ref, wother_ref,
    dq_ref, k_ref, v_ref, w_ref, q_ref, do_ref, x_ref, back_ref, relay_f, relay_b, out_buf, kv_ref, comp_ref, dkv_ref, dcomp_ref, b_buf, b_sum, a_buf,
    doc, dos, dq_acc, bias_c, bias_s, ck, cv, ckt, kt, dc_acc, dkv_acc, delta_c, delta_s,
    kv_send, kv_recv, g_send, g_recv, f_send, f_recv, h_send, h_recv, a_send, a_recv, b_send, b_recv,
    ra_send, ra_recv, rb_send, rb_recv, w_sems, z_sems, in_sems, dq_sems,
):
    me = lax.axis_index("ctx")
    hd = lax.axis_index("head")
    group = me >> 5
    low = me & 31
    partner = {"head": 1 - hd}
    tokens = q_ref.shape[0]
    half = w_ref.shape[1] // 2
    place = me & 31

    k_in = pltpu.make_async_copy(k_hbm, k_ref, in_sems.at[3])
    v_in = pltpu.make_async_copy(v_hbm, v_ref, in_sems.at[4])
    w_in = pltpu.make_async_copy(w_hbm, w_ref, in_sems.at[5])
    k_in.start()
    v_in.start()
    w_in.start()
    x_in = pltpu.make_async_copy(x_hbm, x_ref, in_sems.at[0])
    do_in = pltpu.make_async_copy(do_hbm, do_ref, in_sems.at[1])
    q_in = pltpu.make_async_copy(q_hbm, q_ref, in_sems.at[2])
    x_in.start()
    do_in.start()
    q_in.start()

    barrier = pltpu.get_barrier_semaphore()

    @functools.partial(each, PLANE)
    def _(a):
        @pl.when(a != place)
        def _():
            signal(barrier, at_ctx(me - place + a))

    @functools.partial(each, OUTER)
    def _(g):
        @pl.when(g != group)
        def _():
            signal(barrier, at_ctx(g * LOW + low))

    for p, j, r in REACH:
        @pl.when(me >= r)
        def _():
            signal(barrier, at_ctx(me - r))

        @pl.when(me + r < RANKS)
        def _():
            signal(barrier, at_ctx(me + r))

    signal(barrier, partner)

    own = jnp.concatenate([ck_ref[...].astype(F32), cv_ref[...].astype(F32)], axis=0)
    comp_ref[pl.ds(me, 1)] = own.astype(BF)[None]

    peers = count(
        [me + r < RANKS for _, _, r in REACH] + [me >= r for _, _, r in REACH]
    )
    pl.semaphore_wait(barrier, peers + (PLANE - 1) + (OUTER - 1) + 1)

    def a_copy(a, slot):
        return remote(
            comp_ref.at[slot], comp_ref.at[slot], a_send.at[a], a_recv.at[slot & 31],
            at_ctx(group * LOW + a),
        )

    def b_copy(g, source):
        rows = pl.ds(source * LOW, LOW)
        return remote(
            comp_ref.at[rows], comp_ref.at[rows], b_send.at[g], b_recv.at[source],
            at_ctx(g * LOW + low),
        )

    def relay_copy(p, i, target):
        return remote(
            out_buf.at[p, 2 * i + 1], relay_f.at[p, i], kv_send.at[p, 2 * i + 1], f_recv.at[p, i],
            at_ctx(target),
        )

    def forward_copy(p, i, target):
        return remote(
            relay_f.at[p, i], kv_ref.at[:, p, 2 * i + 1], f_send.at[p, i],
            kv_recv.at[p, 2 * i + 1], at_ctx(target),
        )

    def grad_relay_copy(b, j, target):
        return remote(
            dkv_ref.at[b, j], relay_b.at[b, j >> 1], g_send.at[b, j], h_recv.at[b, j >> 1],
            at_ctx(target),
        )

    def grad_forward_copy(b, i, target):
        return remote(
            relay_b.at[b, i], back_ref.at[b, 2 * i + 1], h_send.at[b, i],
            g_recv.at[b, 2 * i + 1], at_ctx(target),
        )

    def kv_copy(p, j, target):
        return remote(
            out_buf.at[p, j], kv_ref.at[:, p, j], kv_send.at[p, j], kv_recv.at[p, j], at_ctx(target)
        )

    def grad_copy(b, j, target):
        return remote(
            dkv_ref.at[b, j], back_ref.at[b, j], g_send.at[b, j], g_recv.at[b, j], at_ctx(target)
        )

    def rb_copy(g, source):
        return remote(
            dcomp_ref.at[pl.ds(g * LOW, LOW)], b_buf.at[source], rb_send.at[g], rb_recv.at[source],
            at_ctx(g * LOW + low),
        )

    def ra_copy(a, source):
        return remote(
            b_sum.at[a], a_buf.at[source], ra_send.at[a], ra_recv.at[source],
            at_ctx(group * LOW + a),
        )

    theirs = pl.ds(pl.multiple_of((1 - hd) * half, HD), half)
    w_copy = remote(w_ref.at[:, theirs], wother_ref, w_sems.at[0], w_sems.at[1], partner)
    z_copy = remote(dz_ref, dzother_ref, z_sems.at[0], z_sems.at[1], partner)

    def others_low(visit):
        @functools.partial(each, LOW)
        def _(a):
            @pl.when(a != low)
            def _():
                visit(a)

    def outer_where(test, visit):
        @functools.partial(each, OUTER)
        def _(g):
            @pl.when(test(g))
            def _():
                visit(g)

    def owners(b, visit):
        for j in range(PICKS):
            r = jnp.where((b & 1) == 0, reach(0, j), reach(1, j))

            @pl.when(me >= r)
            def _():
                visit(j, me - r)

    def fetch_forwards(p, i, visit):
        r = reach_of(p, 2 * i + 1)
        planes = (place + r) >> 5
        source = me - PLANE * planes
        target = source + r

        @pl.when((planes > 0) & (source >= 0) & (target != me))
        def _():
            visit(target)

    def grad_forwards(b, i, visit):
        r = reach_of(b & 1, 2 * i + 1)
        planes = (r - place + PLANE - 1) >> 5
        source = me + PLANE * planes
        target = source - r

        @pl.when((r > place) & (source < RANKS) & (target != me))
        def _():
            visit(target)

    def send_relayed(q):
        for p, j, r in REACH:
            if p == q and j % 2 == 1 and r % PLANE != 0:
                @pl.when((me + r < RANKS) & crosses(me, me + r))
                def _():
                    relay_copy(p, j // 2, stop(me, me + r)).start()

    def send_direct(q):
        for p, j, r in REACH[q * PICKS:(q + 1) * PICKS]:
            inside = me + r < RANKS
            if j % 2 == 1 and r % PLANE != 0:
                inside = inside & jnp.logical_not(crosses(me, me + r))

            @pl.when(inside)
            def _():
                kv_copy(p, j, me + r).start()

    others_low(lambda a: a_copy(a, me).start())
    @functools.partial(each, OUTER)
    def _(g):
        @pl.when(g > group)
        def _():
            comp_ref[pl.ds(g * LOW, LOW)] = jnp.zeros((LOW, 8, HD), BF)

    k_in.wait()
    v_in.wait()
    def prepare(q):
        for p, j, r in REACH[q * PICKS:(q + 1) * PICKS]:
            asker = jnp.minimum(me + r, RANKS - 1)
            for i in range(2):
                local = sel_ref[j, asker * QB + (p + 2 * i)] & (QB - 1)
                out_buf[p, j, i, :, 0:HD] = k_ref[local]
                out_buf[p, j, i, :, HD:] = v_ref[local]

            @pl.when(me < r)
            def _():
                kv_ref[:, p, j] = jnp.zeros((2, BLK, 2 * HD), BF)

    for b in range(QB):
        kv_ref[b // 2, b % 2, PICKS, :, 0:HD] = k_ref[b]
        kv_ref[b // 2, b % 2, PICKS, :, HD:] = v_ref[b]

    prepare(0)
    send_relayed(0)
    others_low(lambda a: a_copy(a, group * LOW + a).wait_recv())
    outer_where(lambda g: g > group, lambda g: b_copy(g, group).start())
    send_direct(0)
    prepare(1)
    send_relayed(1)
    w_in.wait()
    w_copy.start()

    row = lax.broadcasted_iota(jnp.int32, (RANKS * QB, tokens), 0)
    col = lax.broadcasted_iota(jnp.int32, (RANKS * QB, tokens), 1)
    bias_c[...] = jnp.where(row <= me * QB + (col >> 6), 0.0, -jnp.inf)
    srow = lax.broadcasted_iota(jnp.int32, (BLK, 4 * BLK), 0)
    scol = lax.broadcasted_iota(jnp.int32, (BLK, 4 * BLK), 1) % BLK
    own_bias = jnp.where(srow <= scol, 0.0, -jnp.inf)
    for p, j, r in REACH:
        bias_s[p, j * BLK:(j + 1) * BLK, :] = jnp.full(
            (BLK, 4 * BLK), jnp.where(me >= r, 0.0, -jnp.inf), F32
        )
    for p in range(2):
        bias_s[p, PICKS * BLK:, :] = own_bias
    x_in.wait()
    do_in.wait()
    gate = jax.nn.sigmoid(nt(x_ref[...], w_ref[...]))
    for h in range(HEADS):
        slab = do_ref[:, h * HD:(h + 1) * HD].astype(F32)
        doc[:, h * HD:(h + 1) * HD] = (gate[:, h:h + 1] * slab).astype(BF)
        dos[:, h * HD:(h + 1) * HD] = (gate[:, HEADS + h:HEADS + h + 1] * slab).astype(BF)
    q_in.wait()

    outer_where(lambda g: g < group, lambda g: b_copy(g, g).wait_recv())
    pairs = comp_ref[...].astype(F32).reshape(RANKS // 2, 2, 8, HD)
    even, odd = pairs[:, 0], pairs[:, 1]
    top_rows = lax.broadcasted_iota(jnp.int32, (RANKS // 2, 8, HD), 1) < 4
    swap = lambda z: pltpu.roll(z, 4, 1)
    keys_c = jnp.where(top_rows, even, swap(odd)).reshape(RANKS * 4, HD)
    vals_c = jnp.where(top_rows, swap(even), odd).reshape(RANKS * 4, HD)
    ck[...] = keys_c.astype(BF)
    cv[...] = vals_c.astype(BF)
    ckt[...] = keys_c.T.astype(BF)
    dc_acc[...] = jnp.zeros_like(dc_acc)

    @functools.partial(each, HEADS // 2)
    def _(h2):
        @pl.when(h2 < RELAYS)
        def _():
            for n in range(2):
                h = 2 * h2 + n
                p = (h >= RELAYS).astype(jnp.int32)
                i = h - RELAYS * p

                def pass_on(target):
                    relay_copy(p, i, target).wait_recv()
                    forward_copy(p, i, target).start()

                fetch_forwards(p, i, pass_on)

        @pl.when(h2 == 4)
        def _():
            send_direct(1)

        heads = [pl.ds(pl.multiple_of((2 * h2 + i) * HD, HD), HD) for i in range(2)]
        outs = scores_backward(
            ck[...], cv[...], ckt[...], bias_c[...], [(q_ref[:, l], doc[:, l]) for l in heads]
        )
        for i in range(2):
            dq_acc[:, heads[i]] = outs[i][0].T
            delta_c[pl.ds(2 * h2 + i, 1), :] = outs[i][3]
        dc_acc[0] += outs[0][1] + outs[1][1]
        dc_acc[1] += outs[0][2] + outs[1][2]

    dck = (dc_acc[0] * SCALE).reshape(RANKS // 2, 8, HD)
    dcv = dc_acc[1].reshape(RANKS // 2, 8, HD)
    dcomp_ref[...] = jnp.stack(
        [jnp.where(top_rows, dck, swap(dcv)), jnp.where(top_rows, swap(dck), dcv)], axis=1
    ).reshape(RANKS, 8, HD)
    outer_where(lambda g: g < group, lambda g: rb_copy(g, group).start())

    def dq_out(b):
        rows = pl.ds(pl.multiple_of(b * BLK, BLK), BLK)
        return pltpu.make_async_copy(dq_ref.at[rows], dq_hbm.at[rows], dq_sems.at[b])

    def pass_grads(b):
        @functools.partial(each, RELAYS)
        def _(i):
            def pass_on(target):
                grad_relay_copy(b, 2 * i + 1, target).wait_recv()
                grad_forward_copy(b, i, target).start()

            grad_forwards(b, i, pass_on)

    @functools.partial(each, QB)
    def _(turn):
        b = ((turn & 1) << 1) | (turn >> 1)
        last = ((turn - 1) & 1) << 1 | ((turn - 1) >> 1)

        @pl.when((turn & 1) == 0)
        def _():
            owners(b, lambda j, t: kv_copy(turn >> 1, j, t).wait_recv())

        @pl.when(turn == 2)
        def _():
            b_sum[...] = dcomp_ref[pl.ds(group * LOW, LOW)]

            def add_outer(g):
                rb_copy(g, g).wait_recv()
                b_sum[...] += b_buf[g]

            outer_where(lambda g: g > group, add_outer)
            others_low(lambda a: ra_copy(a, low).start())
            a_buf[pl.ds(low, 1)] = b_sum[pl.ds(low, 1)]

        rows = pl.ds(pl.multiple_of(b * BLK, BLK), BLK)
        keys_all = (PICKS + 1) * BLK
        kt[...] = kv_ref[b >> 1, b & 1, :, :, 0:HD].reshape(keys_all, HD).astype(F32).T.astype(BF)
        dkv_acc[...] = jnp.zeros_like(dkv_acc)
        bias = bias_s.at[b & 1]

        @functools.partial(each, 2)
        def _(g2):
            groups = [2 * g2, 2 * g2 + 1]
            lanes = [[pl.ds(pl.multiple_of((g + 4 * i) * HD, HD), HD) for i in range(4)] for g in groups]
            stack = lambda ref, ls: jnp.concatenate([ref[rows, l] for l in ls], axis=0)
            outs = scores_backward(
                kv_ref[b >> 1, b & 1, :, :, 0:HD].reshape(keys_all, HD),
                kv_ref[b >> 1, b & 1, :, :, HD:].reshape(keys_all, HD),
                kt[...], bias[...], [(stack(q_ref, ls), stack(dos, ls)) for ls in lanes],
            )
            for n in range(2):
                dq = outs[n][0].T
                for i in range(4):
                    total = (dq[i * BLK:(i + 1) * BLK] + dq_acc[rows, lanes[n][i]]) * SCALE
                    dq_ref[rows, lanes[n][i]] = total.astype(BF)
                delta_s[b, pl.ds(groups[n], 1), :] = outs[n][3]
            dkv_acc[:, 0:HD] += outs[0][1] + outs[1][1]
            dkv_acc[:, HD:] += outs[0][2] + outs[1][2]

        factor = jnp.where(
            lax.broadcasted_iota(jnp.int32, (1, 2 * HD), 1) < HD, jnp.float32(SCALE), 1.0
        )
        total = dkv_acc[...] * factor
        dkv_ref[b] = total[0:PICKS * BLK].astype(BF).reshape(PICKS, BLK, 2 * HD)
        down_ref[b] = total[PICKS * BLK:]

        def send_grad(j, t):
            if j % 2 == 0:
                grad_copy(b, j, t).start()
            else:
                hop = crosses(me, t)

                @pl.when(hop)
                def _():
                    grad_relay_copy(b, j, stop(me, t)).start()

                @pl.when(jnp.logical_not(hop))
                def _():
                    grad_copy(b, j, t).start()

        owners(b, send_grad)
        dq_out(b).start()

        @pl.when(turn > 0)
        def _():
            pass_grads(last)

    gate_t = jax.nn.sigmoid(nt(w_ref[...], x_ref[...]))
    dz_ref[0:HEADS, :] = (delta_c[...] * (1.0 - gate_t[0:HEADS])).astype(BF)
    columns = []
    for b in range(QB):
        columns.append(
            jnp.concatenate([delta_s[b, :, i * BLK:(i + 1) * BLK] for i in range(4)], axis=0)
        )
    sel = jnp.concatenate(columns, axis=1)
    dz_ref[HEADS:, :] = (sel * (1.0 - gate_t[HEADS:])).astype(BF)
    z_copy.start()
    pass_grads(QB - 1)

    for b in (0, 2, 1, 3):
        @functools.partial(each, PICKS)
        def _(j):
            t = me + reach_of(b & 1, j)

            @pl.when(t < RANKS)
            def _():
                grad_copy(b, j, t).wait_recv()
                local = sel_ref[j, t * QB + b] & (QB - 1)
                term = back_ref[b, j].astype(F32)
                for c in range(QB):
                    down_ref[c] += jnp.where(local == c, term, 0.0)

    others_low(lambda a: ra_copy(a, a).wait_recv())
    csum_ref[...] = jnp.sum(a_buf[...], axis=0)
    w_copy.wait_recv()
    z_copy.wait_recv()
    each(QB, lambda b: dq_out(b).wait())
    for p, j, r in REACH:
        @pl.when(me + r < RANKS)
        def _():
            kv_copy(p, j, me + r).wait_send()

    for p in range(2):
        @functools.partial(each, RELAYS)
        def _(i):
            fetch_forwards(p, i, lambda t: forward_copy(p, i, t).wait_send())

    @functools.partial(each, QB)
    def _(b):
        owners(b, lambda j, t: grad_copy(b, j, t).wait_send())

    @functools.partial(each, QB)
    def _(b):
        @functools.partial(each, RELAYS)
        def _(i):
            grad_forwards(b, i, lambda t: grad_forward_copy(b, i, t).wait_send())

    others_low(lambda a: a_copy(a, me).wait_send())
    outer_where(lambda g: g > group, lambda g: b_copy(g, group).wait_send())
    outer_where(lambda g: g < group, lambda g: rb_copy(g, group).wait_send())
    others_low(lambda a: ra_copy(a, low).wait_send())
    w_copy.wait_send()
    z_copy.wait_send()


def finish_kernel(
    dq_hbm, down_hbm, csum_hbm, dz_hbm, dzother_hbm, w_hbm, wother_hbm,
    dqo_ref, dk_ref, dv_ref, dck_ref, dcv_ref, dx_ref,
    down_ref, csum_ref, dz_ref, dzother_ref, w_ref, wother_ref, sems,
):
    hd = lax.axis_index("head")
    half = wother_ref.shape[1]
    mine = pl.ds(pl.multiple_of(hd * half, HD), half)
    pairs = [
        (dz_hbm, dz_ref), (dzother_hbm, dzother_ref), (w_hbm.at[:, mine], w_ref),
        (wother_hbm, wother_ref), (down_hbm, down_ref), (csum_hbm, csum_ref), (dq_hbm, dqo_ref),
    ]
    copies = [pltpu.make_async_copy(a, c, sems.at[i]) for i, (a, c) in enumerate(pairs)]
    copies[-1].start()
    for copy in copies[:-1]:
        copy.start()
    for copy in copies[:-1]:
        copy.wait()
    for b in range(QB):
        dk_ref[b * BLK:(b + 1) * BLK, :] = down_ref[b, :, 0:HD].astype(BF)
        dv_ref[b * BLK:(b + 1) * BLK, :] = down_ref[b, :, HD:].astype(BF)
    dck_ref[...] = csum_ref[0:4, :].astype(BF)
    dcv_ref[...] = csum_ref[4:8, :].astype(BF)
    tn = lambda a, c: lax.dot_general(a, c, (((0,), (0,)), ((), ())), preferred_element_type=F32)
    dx_ref[...] = (tn(dz_ref[...], w_ref[...]) + tn(dzother_ref[...], wother_ref[...])).astype(BF)
    copies[-1].wait()


VM = pl.BlockSpec(memory_space=pltpu.VMEM)
SM = pl.BlockSpec(memory_space=pltpu.SMEM)


def body(queries, keys, values, comp_keys, comp_values, selected, inputs, w_gate, d_out):
    tokens = queries.shape[0]
    width = inputs.shape[1]
    half = width // 2
    dma = lambda *n: pltpu.SemaphoreType.DMA(n)
    vm = lambda *shape: pltpu.VMEM(shape, BF)
    vf = lambda *shape: pltpu.VMEM(shape, F32)
    sel = selected.T
    wt = w_gate.T
    keys_all = (PICKS + 1) * BLK
    blocks = (QB, BLK, HD)

    dq, down, csum, dz, dz_other, w_other = pl.pallas_call(
        attention_kernel,
        name="attention",
        out_shape=(
            jax.ShapeDtypeStruct(queries.shape, BF),
            jax.ShapeDtypeStruct((QB, BLK, 2 * HD), F32),
            jax.ShapeDtypeStruct((8, HD), F32),
            jax.ShapeDtypeStruct((2 * HEADS, tokens), BF),
            jax.ShapeDtypeStruct((2 * HEADS, tokens), BF),
            jax.ShapeDtypeStruct((2 * HEADS, half), BF),
        ),
        in_specs=[SM] + [VM] * 2 + [pl.BlockSpec(memory_space=pl.ANY)] * 6,
        out_specs=(pl.BlockSpec(memory_space=pl.ANY),) + (VM,) * 5,
        scratch_shapes=[
            vm(*queries.shape),
            vm(*blocks), vm(*blocks), vm(*wt.shape),
            vm(*queries.shape), vm(*d_out.shape), vm(*inputs.shape),
            vm(QB, PICKS, BLK, 2 * HD),
            vm(2, RELAYS, 2, BLK, 2 * HD), vm(QB, RELAYS, BLK, 2 * HD),
            vm(2, PICKS, 2, BLK, 2 * HD), vm(2, 2, PICKS + 1, BLK, 2 * HD), vm(RANKS, 8, HD),
            vm(QB, PICKS, BLK, 2 * HD), vf(RANKS, 8, HD),
            vf(OUTER, LOW, 8, HD), vf(LOW, 8, HD), vf(LOW, 8, HD),
            vm(*queries.shape), vm(*queries.shape), vf(*queries.shape),
            vf(RANKS * QB, tokens), vf(2, keys_all, 4 * BLK),
            vm(RANKS * QB, HD), vm(RANKS * QB, HD), vm(HD, RANKS * QB), vm(HD, keys_all),
            vf(2, RANKS * QB, HD), vf(keys_all, 2 * HD), vf(HEADS, tokens), vf(QB, 4, 4 * BLK),
            dma(2, PICKS), dma(2, PICKS), dma(QB, PICKS), dma(QB, PICKS),
            dma(2, RELAYS), dma(2, RELAYS), dma(QB, RELAYS), dma(QB, RELAYS),
            dma(LOW), dma(LOW), dma(OUTER), dma(OUTER),
            dma(LOW), dma(LOW), dma(OUTER), dma(OUTER), dma(2), dma(2), dma(6), dma(QB),
        ],
        compiler_params=pltpu.CompilerParams(
            collective_id=0, has_side_effects=True, vmem_limit_bytes=60 * MIB
        ),
    )(
        sel, comp_keys, comp_values, keys.reshape(blocks), values.reshape(blocks), wt,
        queries, d_out, inputs,
    )

    any_space = pl.BlockSpec(memory_space=pl.ANY)
    return pl.pallas_call(
        finish_kernel,
        name="finish",
        out_shape=(
            jax.ShapeDtypeStruct(queries.shape, BF),
            jax.ShapeDtypeStruct((tokens, HD), BF),
            jax.ShapeDtypeStruct((tokens, HD), BF),
            jax.ShapeDtypeStruct((QB, HD), BF),
            jax.ShapeDtypeStruct((QB, HD), BF),
            jax.ShapeDtypeStruct((tokens, half), BF),
        ),
        in_specs=[any_space] * 7,
        out_specs=(VM,) * 6,
        scratch_shapes=[
            vf(QB, BLK, 2 * HD), vf(8, HD), vm(2 * HEADS, tokens), vm(2 * HEADS, tokens),
            vm(2 * HEADS, half), vm(2 * HEADS, half), dma(7),
        ],
        compiler_params=pltpu.CompilerParams(vmem_limit_bytes=60 * MIB),
    )(dq, down, csum, dz, dz_other, wt, w_other)


def solution(mesh):
    split = P("ctx", "head")
    in_specs = (split, split, split, split, split, P(), P("ctx", None), P(None, "head"), split)
    return jax.shard_map(body, mesh=mesh, in_specs=in_specs, out_specs=(split,) * 6, check_vma=False)
```

```python
import functools

import jax
import jax.numpy as jnp
from jax import lax
from jax.experimental import pallas as pl
from jax.experimental.pallas import tpu as pltpu
from jax.sharding import PartitionSpec as P

BLK = 64
PICKS = 15
HD = 128
QB = 4
RANKS = 128
HEADS = 16
LOW = 32
OUTER = RANKS // LOW
HALF = RANKS // 2
PLANE = 32
RELAYS = PICKS // 2
SCALE = HD ** -0.5
LOG2E = 1.4426950408889634
BF = jnp.bfloat16
F32 = jnp.float32
MIB = 1 << 20


def reach(parity, j):
    if parity == 0:
        return 1 + (j * (HALF - 1)) // (PICKS - 1)
    return HALF + 1 + (j * (HALF - 2)) // (PICKS - 1)


REACH = [(p, j, reach(p, j)) for p in range(2) for j in range(PICKS)]


def count(conditions):
    return sum(c.astype(jnp.int32) for c in conditions)


def at_ctx(index):
    return {"ctx": index}


def signal(sem, device):
    pl.semaphore_signal(sem, inc=1, device_id=device, device_id_type=pl.DeviceIdType.MESH)


def remote(src, dst, send_sem, recv_sem, device):
    return pltpu.make_async_remote_copy(
        src_ref=src,
        dst_ref=dst,
        send_sem=send_sem,
        recv_sem=recv_sem,
        device_id=device,
        device_id_type=pl.DeviceIdType.MESH,
    )


def nt(a, b):
    return lax.dot_general(a, b, (((1,), (1,)), ((), ())), preferred_element_type=F32)


def nn(a, b):
    return lax.dot_general(a, b, (((1,), (0,)), ((), ())), preferred_element_type=F32)


def scores_backward(k, v, kt, bias, pairs):
    s = [nt(k, q) * (SCALE * LOG2E) + bias for q, _ in pairs]
    dp = [nt(v, do) for _, do in pairs]
    outs = []
    for i, (q, do) in enumerate(pairs):
        top = jnp.max(s[i], axis=0, keepdims=True)
        e = jnp.exp2(s[i] - top)
        prob = e * (1.0 / jnp.sum(e, axis=0, keepdims=True))
        delta = jnp.sum(prob * dp[i], axis=0, keepdims=True)
        ds = (prob * (dp[i] - delta)).astype(BF)
        dv = nn(prob.astype(BF), do)
        dk = nn(ds, q)
        dqt = nn(kt, ds)
        outs.append((dqt, dk, dv, delta))
    return outs


def reach_of(parity, j):
    return jnp.where(parity == 0, 1 + ((j * 9) >> 1), HALF + 1 + ((j * 31 * 9363) >> 16))


for _p, _j, _r in REACH:
    assert _r == (1 + ((_j * 9) >> 1) if _p == 0 else HALF + 1 + ((_j * 31 * 9363) >> 16))


def crosses(source, target):
    return ((source >> 5) != (target >> 5)) & ((source & 31) != (target & 31))


def stop(source, target):
    return (target & ~31) | (source & 31)


def each(n, visit):
    def step(i, carry):
        visit(i)
        return carry

    lax.fori_loop(0, n, step, 0)


def attention_kernel(
    sel_ref, ck_ref, cv_ref, k_hbm, v_hbm, w_hbm, q_hbm, do_hbm, x_hbm,
    dq_hbm, down_ref, csum_ref, dz_ref, dzother_ref, wother_ref,
    dq_ref, k_ref, v_ref, w_ref, q_ref, do_ref, x_ref, back_ref, relay_f, relay_b, out_buf, kv_ref, comp_ref, dkv_ref, dcomp_ref, b_buf, b_sum, a_buf,
    doc, dos, dq_acc, bias_c, bias_s, ck, cv, ckt, kt, dc_acc, dkv_acc, delta_c, delta_s,
    kv_send, kv_recv, g_send, g_recv, f_send, f_recv, h_send, h_recv, a_send, a_recv, b_send, b_recv,
    ra_send, ra_recv, rb_send, rb_recv, w_sems, z_sems, in_sems, dq_sems,
):
    me = lax.axis_index("ctx")
    hd = lax.axis_index("head")
    group = me >> 5
    low = me & 31
    partner = {"head": 1 - hd}
    tokens = q_ref.shape[0]
    half = w_ref.shape[1] // 2
    place = me & 31

    k_in = pltpu.make_async_copy(k_hbm, k_ref, in_sems.at[3])
    v_in = pltpu.make_async_copy(v_hbm, v_ref, in_sems.at[4])
    w_in = pltpu.make_async_copy(w_hbm, w_ref, in_sems.at[5])
    k_in.start()
    v_in.start()
    w_in.start()
    x_in = pltpu.make_async_copy(x_hbm, x_ref, in_sems.at[0])
    do_in = pltpu.make_async_copy(do_hbm, do_ref, in_sems.at[1])
    q_in = pltpu.make_async_copy(q_hbm, q_ref, in_sems.at[2])
    x_in.start()
    do_in.start()
    q_in.start()

    barrier = pltpu.get_barrier_semaphore()

    @functools.partial(each, PLANE)
    def _(a):
        @pl.when(a != place)
        def _():
            signal(barrier, at_ctx(me - place + a))

    @functools.partial(each, OUTER)
    def _(g):
        @pl.when(g != group)
        def _():
            signal(barrier, at_ctx(g * LOW + low))

    for p, j, r in REACH:
        @pl.when(me >= r)
        def _():
            signal(barrier, at_ctx(me - r))

        @pl.when(me + r < RANKS)
        def _():
            signal(barrier, at_ctx(me + r))

    signal(barrier, partner)

    own = jnp.concatenate([ck_ref[...].astype(F32), cv_ref[...].astype(F32)], axis=0)
    comp_ref[pl.ds(me, 1)] = own.astype(BF)[None]

    peers = count(
        [me + r < RANKS for _, _, r in REACH] + [me >= r for _, _, r in REACH]
    )
    pl.semaphore_wait(barrier, peers + (PLANE - 1) + (OUTER - 1) + 1)

    def a_copy(a, slot):
        return remote(
            comp_ref.at[slot], comp_ref.at[slot], a_send.at[a], a_recv.at[slot & 31],
            at_ctx(group * LOW + a),
        )

    def b_copy(g, source):
        rows = pl.ds(source * LOW, LOW)
        return remote(
            comp_ref.at[rows], comp_ref.at[rows], b_send.at[g], b_recv.at[source],
            at_ctx(g * LOW + low),
        )

    def relay_copy(p, i, target):
        return remote(
            out_buf.at[p, 2 * i + 1], relay_f.at[p, i], kv_send.at[p, 2 * i + 1], f_recv.at[p, i],
            at_ctx(target),
        )

    def forward_copy(p, i, target):
        return remote(
            relay_f.at[p, i], kv_ref.at[:, p, 2 * i + 1], f_send.at[p, i],
            kv_recv.at[p, 2 * i + 1], at_ctx(target),
        )

    def grad_relay_copy(b, j, target):
        return remote(
            dkv_ref.at[b, j], relay_b.at[b, j >> 1], g_send.at[b, j], h_recv.at[b, j >> 1],
            at_ctx(target),
        )

    def grad_forward_copy(b, i, target):
        return remote(
            relay_b.at[b, i], back_ref.at[b, 2 * i + 1], h_send.at[b, i],
            g_recv.at[b, 2 * i + 1], at_ctx(target),
        )

    def kv_copy(p, j, target):
        return remote(
            out_buf.at[p, j], kv_ref.at[:, p, j], kv_send.at[p, j], kv_recv.at[p, j], at_ctx(target)
        )

    def grad_copy(b, j, target):
        return remote(
            dkv_ref.at[b, j], back_ref.at[b, j], g_send.at[b, j], g_recv.at[b, j], at_ctx(target)
        )

    def rb_copy(g, source):
        return remote(
            dcomp_ref.at[pl.ds(g * LOW, LOW)], b_buf.at[source], rb_send.at[g], rb_recv.at[source],
            at_ctx(g * LOW + low),
        )

    def ra_copy(a, source):
        return remote(
            b_sum.at[a], a_buf.at[source], ra_send.at[a], ra_recv.at[source],
            at_ctx(group * LOW + a),
        )

    theirs = pl.ds(pl.multiple_of((1 - hd) * half, HD), half)
    w_copy = remote(w_ref.at[:, theirs], wother_ref, w_sems.at[0], w_sems.at[1], partner)
    z_copy = remote(dz_ref, dzother_ref, z_sems.at[0], z_sems.at[1], partner)

    def others_low(visit):
        @functools.partial(each, LOW)
        def _(a):
            @pl.when(a != low)
            def _():
                visit(a)

    def outer_where(test, visit):
        @functools.partial(each, OUTER)
        def _(g):
            @pl.when(test(g))
            def _():
                visit(g)

    def owners(b, visit):
        for j in range(PICKS):
            r = jnp.where((b & 1) == 0, reach(0, j), reach(1, j))

            @pl.when(me >= r)
            def _():
                visit(j, me - r)

    def fetch_forwards(p, i, visit):
        r = reach_of(p, 2 * i + 1)
        planes = (place + r) >> 5
        source = me - PLANE * planes
        target = source + r

        @pl.when((planes > 0) & (source >= 0) & (target != me))
        def _():
            visit(target)

    def grad_forwards(b, i, visit):
        r = reach_of(b & 1, 2 * i + 1)
        planes = (r - place + PLANE - 1) >> 5
        source = me + PLANE * planes
        target = source - r

        @pl.when((r > place) & (source < RANKS) & (target != me))
        def _():
            visit(target)

    def send_relayed(q):
        for p, j, r in REACH:
            if p == q and j % 2 == 1 and r % PLANE != 0:
                @pl.when((me + r < RANKS) & crosses(me, me + r))
                def _():
                    relay_copy(p, j // 2, stop(me, me + r)).start()

    def send_direct(q):
        for p, j, r in REACH[q * PICKS:(q + 1) * PICKS]:
            inside = me + r < RANKS
            if j % 2 == 1 and r % PLANE != 0:
                inside = inside & jnp.logical_not(crosses(me, me + r))

            @pl.when(inside)
            def _():
                kv_copy(p, j, me + r).start()

    others_low(lambda a: a_copy(a, me).start())
    @functools.partial(each, OUTER)
    def _(g):
        @pl.when(g > group)
        def _():
            comp_ref[pl.ds(g * LOW, LOW)] = jnp.zeros((LOW, 8, HD), BF)

    k_in.wait()
    v_in.wait()
    def prepare(q):
        for p, j, r in REACH[q * PICKS:(q + 1) * PICKS]:
            asker = jnp.minimum(me + r, RANKS - 1)
            for i in range(2):
                local = sel_ref[j, asker * QB + (p + 2 * i)] & (QB - 1)
                out_buf[p, j, i, :, 0:HD] = k_ref[local]
                out_buf[p, j, i, :, HD:] = v_ref[local]

            @pl.when(me < r)
            def _():
                kv_ref[:, p, j] = jnp.zeros((2, BLK, 2 * HD), BF)

    for b in range(QB):
        kv_ref[b // 2, b % 2, PICKS, :, 0:HD] = k_ref[b]
        kv_ref[b // 2, b % 2, PICKS, :, HD:] = v_ref[b]

    prepare(0)
    send_relayed(0)
    others_low(lambda a: a_copy(a, group * LOW + a).wait_recv())
    outer_where(lambda g: g > group, lambda g: b_copy(g, group).start())
    send_direct(0)
    prepare(1)
    send_relayed(1)
    w_in.wait()
    w_copy.start()

    row = lax.broadcasted_iota(jnp.int32, (RANKS * QB, tokens), 0)
    col = lax.broadcasted_iota(jnp.int32, (RANKS * QB, tokens), 1)
    bias_c[...] = jnp.where(row <= me * QB + (col >> 6), 0.0, -jnp.inf)
    srow = lax.broadcasted_iota(jnp.int32, (BLK, 4 * BLK), 0)
    scol = lax.broadcasted_iota(jnp.int32, (BLK, 4 * BLK), 1) % BLK
    own_bias = jnp.where(srow <= scol, 0.0, -jnp.inf)
    for p, j, r in REACH:
        bias_s[p, j * BLK:(j + 1) * BLK, :] = jnp.full(
            (BLK, 4 * BLK), jnp.where(me >= r, 0.0, -jnp.inf), F32
        )
    for p in range(2):
        bias_s[p, PICKS * BLK:, :] = own_bias
    x_in.wait()
    do_in.wait()
    gate = jax.nn.sigmoid(nt(x_ref[...], w_ref[...]))
    for h in range(HEADS):
        slab = do_ref[:, h * HD:(h + 1) * HD].astype(F32)
        doc[:, h * HD:(h + 1) * HD] = (gate[:, h:h + 1] * slab).astype(BF)
        dos[:, h * HD:(h + 1) * HD] = (gate[:, HEADS + h:HEADS + h + 1] * slab).astype(BF)
    q_in.wait()

    outer_where(lambda g: g < group, lambda g: b_copy(g, g).wait_recv())
    pairs = comp_ref[...].astype(F32).reshape(RANKS // 2, 2, 8, HD)
    even, odd = pairs[:, 0], pairs[:, 1]
    top_rows = lax.broadcasted_iota(jnp.int32, (RANKS // 2, 8, HD), 1) < 4
    swap = lambda z: pltpu.roll(z, 4, 1)
    keys_c = jnp.where(top_rows, even, swap(odd)).reshape(RANKS * 4, HD)
    vals_c = jnp.where(top_rows, swap(even), odd).reshape(RANKS * 4, HD)
    ck[...] = keys_c.astype(BF)
    cv[...] = vals_c.astype(BF)
    ckt[...] = keys_c.T.astype(BF)
    dc_acc[...] = jnp.zeros_like(dc_acc)

    @functools.partial(each, HEADS // 2)
    def _(h2):
        def pass_keys(p, i):
            def pass_on(target):
                relay_copy(p, i, target).wait_recv()
                forward_copy(p, i, target).start()

            @pl.when(i < RELAYS)
            def _():
                fetch_forwards(p, i, pass_on)

        @pl.when(h2 < 2)
        def _():
            for n in range(4):
                pass_keys(0, 4 * h2 + n)

        @pl.when(h2 >= 4)
        def _():
            for n in range(2):
                pass_keys(1, 2 * (h2 - 4) + n)

        @pl.when(h2 == 4)
        def _():
            send_direct(1)

        heads = [pl.ds(pl.multiple_of((2 * h2 + i) * HD, HD), HD) for i in range(2)]
        outs = scores_backward(
            ck[...], cv[...], ckt[...], bias_c[...], [(q_ref[:, l], doc[:, l]) for l in heads]
        )
        for i in range(2):
            dq_acc[:, heads[i]] = outs[i][0].T
            delta_c[pl.ds(2 * h2 + i, 1), :] = outs[i][3]
        dc_acc[0] += outs[0][1] + outs[1][1]
        dc_acc[1] += outs[0][2] + outs[1][2]

    dck = (dc_acc[0] * SCALE).reshape(RANKS // 2, 8, HD)
    dcv = dc_acc[1].reshape(RANKS // 2, 8, HD)
    dcomp_ref[...] = jnp.stack(
        [jnp.where(top_rows, dck, swap(dcv)), jnp.where(top_rows, swap(dck), dcv)], axis=1
    ).reshape(RANKS, 8, HD)
    outer_where(lambda g: g < group, lambda g: rb_copy(g, group).start())

    def dq_out(b):
        rows = pl.ds(pl.multiple_of(b * BLK, BLK), BLK)
        return pltpu.make_async_copy(dq_ref.at[rows], dq_hbm.at[rows], dq_sems.at[b])

    def pass_grads(b):
        @functools.partial(each, RELAYS)
        def _(i):
            def pass_on(target):
                grad_relay_copy(b, 2 * i + 1, target).wait_recv()
                grad_forward_copy(b, i, target).start()

            grad_forwards(b, i, pass_on)

    @functools.partial(each, QB)
    def _(turn):
        b = ((turn & 1) << 1) | (turn >> 1)
        last = ((turn - 1) & 1) << 1 | ((turn - 1) >> 1)

        @pl.when((turn & 1) == 0)
        def _():
            owners(b, lambda j, t: kv_copy(turn >> 1, j, t).wait_recv())

        @pl.when(turn == 2)
        def _():
            b_sum[...] = dcomp_ref[pl.ds(group * LOW, LOW)]

            def add_outer(g):
                rb_copy(g, g).wait_recv()
                b_sum[...] += b_buf[g]

            outer_where(lambda g: g > group, add_outer)
            others_low(lambda a: ra_copy(a, low).start())
            a_buf[pl.ds(low, 1)] = b_sum[pl.ds(low, 1)]

        rows = pl.ds(pl.multiple_of(b * BLK, BLK), BLK)
        keys_all = (PICKS + 1) * BLK
        kt[...] = kv_ref[b >> 1, b & 1, :, :, 0:HD].reshape(keys_all, HD).astype(F32).T.astype(BF)
        dkv_acc[...] = jnp.zeros_like(dkv_acc)
        bias = bias_s.at[b & 1]

        @functools.partial(each, 2)
        def _(g2):
            groups = [2 * g2, 2 * g2 + 1]
            lanes = [[pl.ds(pl.multiple_of((g + 4 * i) * HD, HD), HD) for i in range(4)] for g in groups]
            stack = lambda ref, ls: jnp.concatenate([ref[rows, l] for l in ls], axis=0)
            outs = scores_backward(
                kv_ref[b >> 1, b & 1, :, :, 0:HD].reshape(keys_all, HD),
                kv_ref[b >> 1, b & 1, :, :, HD:].reshape(keys_all, HD),
                kt[...], bias[...], [(stack(q_ref, ls), stack(dos, ls)) for ls in lanes],
            )
            for n in range(2):
                dq = outs[n][0].T
                for i in range(4):
                    total = (dq[i * BLK:(i + 1) * BLK] + dq_acc[rows, lanes[n][i]]) * SCALE
                    dq_ref[rows, lanes[n][i]] = total.astype(BF)
                delta_s[b, pl.ds(groups[n], 1), :] = outs[n][3]
            dkv_acc[:, 0:HD] += outs[0][1] + outs[1][1]
            dkv_acc[:, HD:] += outs[0][2] + outs[1][2]

        factor = jnp.where(
            lax.broadcasted_iota(jnp.int32, (1, 2 * HD), 1) < HD, jnp.float32(SCALE), 1.0
        )
        total = dkv_acc[...] * factor
        dkv_ref[b] = total[0:PICKS * BLK].astype(BF).reshape(PICKS, BLK, 2 * HD)
        down_ref[b] = total[PICKS * BLK:]

        def send_grad(j, t):
            if j % 2 == 0:
                grad_copy(b, j, t).start()
            else:
                hop = crosses(me, t)

                @pl.when(hop)
                def _():
                    grad_relay_copy(b, j, stop(me, t)).start()

                @pl.when(jnp.logical_not(hop))
                def _():
                    grad_copy(b, j, t).start()

        owners(b, send_grad)
        dq_out(b).start()

        @pl.when(turn > 0)
        def _():
            pass_grads(last)

    gate_t = jax.nn.sigmoid(nt(w_ref[...], x_ref[...]))
    dz_ref[0:HEADS, :] = (delta_c[...] * (1.0 - gate_t[0:HEADS])).astype(BF)
    columns = []
    for b in range(QB):
        columns.append(
            jnp.concatenate([delta_s[b, :, i * BLK:(i + 1) * BLK] for i in range(4)], axis=0)
        )
    sel = jnp.concatenate(columns, axis=1)
    dz_ref[HEADS:, :] = (sel * (1.0 - gate_t[HEADS:])).astype(BF)
    z_copy.start()
    pass_grads(QB - 1)

    for b in (0, 2, 1, 3):
        @functools.partial(each, PICKS)
        def _(j):
            t = me + reach_of(b & 1, j)

            @pl.when(t < RANKS)
            def _():
                grad_copy(b, j, t).wait_recv()
                local = sel_ref[j, t * QB + b] & (QB - 1)
                term = back_ref[b, j].astype(F32)
                for c in range(QB):
                    down_ref[c] += jnp.where(local == c, term, 0.0)

    others_low(lambda a: ra_copy(a, a).wait_recv())
    csum_ref[...] = jnp.sum(a_buf[...], axis=0)
    w_copy.wait_recv()
    z_copy.wait_recv()
    each(QB, lambda b: dq_out(b).wait())
    for p, j, r in REACH:
        @pl.when(me + r < RANKS)
        def _():
            kv_copy(p, j, me + r).wait_send()

    for p in range(2):
        @functools.partial(each, RELAYS)
        def _(i):
            fetch_forwards(p, i, lambda t: forward_copy(p, i, t).wait_send())

    @functools.partial(each, QB)
    def _(b):
        owners(b, lambda j, t: grad_copy(b, j, t).wait_send())

    @functools.partial(each, QB)
    def _(b):
        @functools.partial(each, RELAYS)
        def _(i):
            grad_forwards(b, i, lambda t: grad_forward_copy(b, i, t).wait_send())

    others_low(lambda a: a_copy(a, me).wait_send())
    outer_where(lambda g: g > group, lambda g: b_copy(g, group).wait_send())
    outer_where(lambda g: g < group, lambda g: rb_copy(g, group).wait_send())
    others_low(lambda a: ra_copy(a, low).wait_send())
    w_copy.wait_send()
    z_copy.wait_send()


def finish_kernel(
    dq_hbm, down_hbm, csum_hbm, dz_hbm, dzother_hbm, w_hbm, wother_hbm,
    dqo_ref, dk_ref, dv_ref, dck_ref, dcv_ref, dx_ref,
    down_ref, csum_ref, dz_ref, dzother_ref, w_ref, wother_ref, sems,
):
    hd = lax.axis_index("head")
    half = wother_ref.shape[1]
    mine = pl.ds(pl.multiple_of(hd * half, HD), half)
    pairs = [
        (dz_hbm, dz_ref), (dzother_hbm, dzother_ref), (w_hbm.at[:, mine], w_ref),
        (wother_hbm, wother_ref), (down_hbm, down_ref), (csum_hbm, csum_ref), (dq_hbm, dqo_ref),
    ]
    copies = [pltpu.make_async_copy(a, c, sems.at[i]) for i, (a, c) in enumerate(pairs)]
    copies[-1].start()
    for copy in copies[:-1]:
        copy.start()
    for copy in copies[:-1]:
        copy.wait()
    for b in range(QB):
        dk_ref[b * BLK:(b + 1) * BLK, :] = down_ref[b, :, 0:HD].astype(BF)
        dv_ref[b * BLK:(b + 1) * BLK, :] = down_ref[b, :, HD:].astype(BF)
    dck_ref[...] = csum_ref[0:4, :].astype(BF)
    dcv_ref[...] = csum_ref[4:8, :].astype(BF)
    tn = lambda a, c: lax.dot_general(a, c, (((0,), (0,)), ((), ())), preferred_element_type=F32)
    dx_ref[...] = (tn(dz_ref[...], w_ref[...]) + tn(dzother_ref[...], wother_ref[...])).astype(BF)
    copies[-1].wait()


VM = pl.BlockSpec(memory_space=pltpu.VMEM)
SM = pl.BlockSpec(memory_space=pltpu.SMEM)


def body(queries, keys, values, comp_keys, comp_values, selected, inputs, w_gate, d_out):
    tokens = queries.shape[0]
    width = inputs.shape[1]
    half = width // 2
    dma = lambda *n: pltpu.SemaphoreType.DMA(n)
    vm = lambda *shape: pltpu.VMEM(shape, BF)
    vf = lambda *shape: pltpu.VMEM(shape, F32)
    sel = selected.T
    wt = w_gate.T
    keys_all = (PICKS + 1) * BLK
    blocks = (QB, BLK, HD)

    dq, down, csum, dz, dz_other, w_other = pl.pallas_call(
        attention_kernel,
        name="attention",
        out_shape=(
            jax.ShapeDtypeStruct(queries.shape, BF),
            jax.ShapeDtypeStruct((QB, BLK, 2 * HD), F32),
            jax.ShapeDtypeStruct((8, HD), F32),
            jax.ShapeDtypeStruct((2 * HEADS, tokens), BF),
            jax.ShapeDtypeStruct((2 * HEADS, tokens), BF),
            jax.ShapeDtypeStruct((2 * HEADS, half), BF),
        ),
        in_specs=[SM] + [VM] * 2 + [pl.BlockSpec(memory_space=pl.ANY)] * 6,
        out_specs=(pl.BlockSpec(memory_space=pl.ANY),) + (VM,) * 5,
        scratch_shapes=[
            vm(*queries.shape),
            vm(*blocks), vm(*blocks), vm(*wt.shape),
            vm(*queries.shape), vm(*d_out.shape), vm(*inputs.shape),
            vm(QB, PICKS, BLK, 2 * HD),
            vm(2, RELAYS, 2, BLK, 2 * HD), vm(QB, RELAYS, BLK, 2 * HD),
            vm(2, PICKS, 2, BLK, 2 * HD), vm(2, 2, PICKS + 1, BLK, 2 * HD), vm(RANKS, 8, HD),
            vm(QB, PICKS, BLK, 2 * HD), vf(RANKS, 8, HD),
            vf(OUTER, LOW, 8, HD), vf(LOW, 8, HD), vf(LOW, 8, HD),
            vm(*queries.shape), vm(*queries.shape), vf(*queries.shape),
            vf(RANKS * QB, tokens), vf(2, keys_all, 4 * BLK),
            vm(RANKS * QB, HD), vm(RANKS * QB, HD), vm(HD, RANKS * QB), vm(HD, keys_all),
            vf(2, RANKS * QB, HD), vf(keys_all, 2 * HD), vf(HEADS, tokens), vf(QB, 4, 4 * BLK),
            dma(2, PICKS), dma(2, PICKS), dma(QB, PICKS), dma(QB, PICKS),
            dma(2, RELAYS), dma(2, RELAYS), dma(QB, RELAYS), dma(QB, RELAYS),
            dma(LOW), dma(LOW), dma(OUTER), dma(OUTER),
            dma(LOW), dma(LOW), dma(OUTER), dma(OUTER), dma(2), dma(2), dma(6), dma(QB),
        ],
        compiler_params=pltpu.CompilerParams(
            collective_id=0, has_side_effects=True, vmem_limit_bytes=60 * MIB
        ),
    )(
        sel, comp_keys, comp_values, keys.reshape(blocks), values.reshape(blocks), wt,
        queries, d_out, inputs,
    )

    any_space = pl.BlockSpec(memory_space=pl.ANY)
    return pl.pallas_call(
        finish_kernel,
        name="finish",
        out_shape=(
            jax.ShapeDtypeStruct(queries.shape, BF),
            jax.ShapeDtypeStruct((tokens, HD), BF),
            jax.ShapeDtypeStruct((tokens, HD), BF),
            jax.ShapeDtypeStruct((QB, HD), BF),
            jax.ShapeDtypeStruct((QB, HD), BF),
            jax.ShapeDtypeStruct((tokens, half), BF),
        ),
        in_specs=[any_space] * 7,
        out_specs=(VM,) * 6,
        scratch_shapes=[
            vf(QB, BLK, 2 * HD), vf(8, HD), vm(2 * HEADS, tokens), vm(2 * HEADS, tokens),
            vm(2 * HEADS, half), vm(2 * HEADS, half), dma(7),
        ],
        compiler_params=pltpu.CompilerParams(vmem_limit_bytes=60 * MIB),
    )(dq, down, csum, dz, dz_other, wt, w_other)


def solution(mesh):
    split = P("ctx", "head")
    in_specs = (split, split, split, split, split, P(), P("ctx", None), P(None, "head"), split)
    return jax.shard_map(body, mesh=mesh, in_specs=in_specs, out_specs=(split,) * 6, check_vma=False)
```
